32 devices in a mesh: rows: 16 (over z, y, x), rep: 2 (over core).
Axes of the slice: x: 2, y: 2, z: 4, core: 2. Of those that a mesh axis runs over, the one named last changes fastest.
Arguments:
- entity_table: bfloat16 [98304, 256], P('rows'), may hold values from -3 to 3
- relation_ops: bfloat16 [8, 256, 256], replicated, may hold values from -0.375 to 0.375
- need_rows: int32 [16, 2, 16, 8], P('rows', 'rep'), may hold values from 0 to 6143
- send_offsets: int32 [16, 2, 17], P('rows', 'rep'), may hold values from 0 to 128, as said below
- source_ids: int32 [16, 2, 2, 1024], P('rows', 'rep'), may hold values from 0 to 127, as said below
- target_ids: int32 [16, 2, 2, 1024], P('rows', 'rep'), may hold values from 0 to 127, as said below
- negative_ids: int32 [16, 2, 2, 1024], P('rows', 'rep'), may hold values from 0 to 127, as said below
- relation_ids: int32 [16, 2, 2], P('rows', 'rep'), may hold values from 0 to 7
Outputs:
- entity_grad: bfloat16 [98304, 256], P(('rows', 'rep'))
- relation_grad: float32 [8, 256, 256], replicated
The draws below stay inside these ranges and needn't reach their ends.
Inputs may be any that keep to these rules, and one draw needn't show every extreme that they name: `send_offsets`: along the last dimension the offsets start at 0 and rise by 2 to 8 from owner to owner; there is one owner, the same for every device, from which every device requests exactly 8 rows (rise of 8), and there is one device that requests 8 rows from every owner. `source_ids`: each id is below the device's last entry of send_offsets; on every device some id is 0 and some id is that last entry minus 1. `target_ids`: each id is below the device's last entry of send_offsets; on every device some id is 0 and some id is that last entry minus 1. `negative_ids`: each id is below the device's last entry of send_offsets; on every device some id is 0 and some id is that last entry minus 1. `need_rows`: entries past an owner's count of requested rows are not referenced.
All inputs are finite; a program needn't handle non-finite values.
Results may differ from the reference program's by a relative error of at most 0.0065.
Values may be sent and summed in bfloat16 or wider, within the bound.
A program may use at most 64 MiB of HBM per device.

```python
import jax
import jax.numpy as jnp
from jax import lax

EMBED_DIM = 256
RELATIONS = 8
ROWS_DEV = 6144
CAPACITY = 8
EDGES = 1024
NEGATIVES = 1024
BLOCKS = 2
ENTITIES = 98304
N_ROWS = 16
N_REP = 2


def plan_counts(key):
    base_count = jax.random.randint(jax.random.fold_in(key, 11), (N_ROWS, N_REP, N_ROWS), CAPACITY // 4, 3 * CAPACITY // 4 + 1)
    owner_heat = jax.random.randint(jax.random.fold_in(key, 12), (N_ROWS,), 0, 4)
    hot_owner = jax.random.randint(jax.random.fold_in(key, 13), (), 0, N_ROWS)
    full_device = jax.random.randint(jax.random.fold_in(key, 14), (), 0, N_ROWS * N_REP)
    counts = jnp.minimum(base_count + owner_heat[None, None, :] * (CAPACITY // 8), CAPACITY)
    owner_index = jnp.arange(N_ROWS, dtype=jnp.int32)
    counts = jnp.where(owner_index[None, None, :] == hot_owner, CAPACITY, counts)
    device_index = jnp.arange(N_ROWS * N_REP, dtype=jnp.int32).reshape(N_ROWS, N_REP)
    counts = jnp.where((device_index == full_device)[:, :, None], CAPACITY, counts)
    return counts.astype(jnp.int32)


def draw_send_offsets(key, part):
    counts = plan_counts(key)
    leading = jnp.zeros((N_ROWS, N_REP, 1), jnp.int32)
    return jnp.concatenate([leading, jnp.cumsum(counts, axis=-1).astype(jnp.int32)], axis=-1).astype(jnp.int32)


def draw_compact(key, salt, length):
    totals = jnp.sum(plan_counts(key), axis=-1).astype(jnp.int32)
    drawn = jax.random.randint(jax.random.fold_in(key, salt), (N_ROWS, N_REP, BLOCKS, length), 0, totals[:, :, None, None]).astype(jnp.int32)
    drawn = drawn.at[:, :, 0, 0].set(totals - 1)
    drawn = drawn.at[:, :, 0, 1].set(0)
    return drawn.astype(jnp.int32)


def draw_source_ids(key, part):
    return draw_compact(key, 21, EDGES)


def draw_target_ids(key, part):
    return draw_compact(key, 22, EDGES)


def draw_negative_ids(key, part):
    return draw_compact(key, 23, NEGATIVES)


def place_ends(array, key, low, high):
    shape = array.shape
    place = [jax.random.randint(jax.random.fold_in(key, axis), (), 0, shape[axis]) for axis in range(len(shape))]
    array = array.at[tuple(place)].set(low)
    longest = shape.index(max(shape))
    place[longest] = (place[longest] + 1) % shape[longest]
    return array.at[tuple(place)].set(high)


def shard_levels(key, shape, pieces, smallest, high):
    loudness, own = 1.0, jax.random.fold_in(key, 6)
    for dim, blocks in pieces:
        steps = jnp.exp(jax.random.uniform(jax.random.fold_in(own, dim), (blocks,), jnp.float32, smallest / len(pieces), high / len(pieces)))
        loudness = loudness * jnp.repeat(steps, shape[dim] // blocks).reshape([-1 if axis == dim else 1 for axis in range(len(shape))])
    return loudness


def gaussian(own_key, shape, scale, bound, split=(), kind=jnp.bfloat16):
    level = shard_levels(own_key, shape, split, -0.22, 0.18) if split else 1.0
    result = jax.random.normal(own_key, shape, jnp.float32) * scale * level
    return jnp.minimum(jnp.maximum(result, -bound), bound).astype(kind)


def setup_inputs(seed: int = 0) -> dict:
    key_list = jax.random.split(jax.random.key(seed), 9)
    entity_table = gaussian(key_list[0], (ENTITIES, EMBED_DIM), 0.5, 3.0, ((0, 16),))
    relation_ops = gaussian(key_list[1], (RELATIONS, EMBED_DIM, EMBED_DIM), EMBED_DIM ** -0.5, 0.375)
    need_rows = place_ends(jax.random.randint(key_list[2], (N_ROWS, N_REP, N_ROWS, CAPACITY), 0, ROWS_DEV), jax.random.fold_in(key_list[2], 1), 0, ROWS_DEV - 1).astype(jnp.int32)
    send_offsets = draw_send_offsets(jax.random.fold_in(key_list[8], 71), 0)
    source_ids = draw_source_ids(jax.random.fold_in(key_list[8], 71), 0)
    target_ids = draw_target_ids(jax.random.fold_in(key_list[8], 71), 0)
    negative_ids = draw_negative_ids(jax.random.fold_in(key_list[8], 71), 0)
    relation_ids = place_ends(jax.random.randint(key_list[7], (N_ROWS, N_REP, BLOCKS), 0, RELATIONS), jax.random.fold_in(key_list[7], 1), 0, RELATIONS - 1).astype(jnp.int32)
    return dict(entity_table=entity_table, relation_ops=relation_ops, need_rows=need_rows, send_offsets=send_offsets, source_ids=source_ids, target_ids=target_ids, negative_ids=negative_ids, relation_ids=relation_ids)


def locate(edge_ids, offsets, capacity):
    upper_bound = offsets[1:]
    lower_bound = offsets[:-1]
    owner_index = jnp.sum((edge_ids[..., None] >= upper_bound).astype(jnp.int32), axis=-1)
    start_slot = jnp.max(jnp.where(edge_ids[..., None] >= lower_bound, lower_bound, 0), axis=-1)
    return (owner_index * capacity + edge_ids - start_slot).astype(jnp.int32)


def block_terms(slots, operator, source_slot, target_slot, negative_slot, weight_neg):
    source = jnp.take(slots, source_slot, axis=0)
    target = jnp.take(slots, target_slot, axis=0)
    negative = jnp.take(slots, negative_slot, axis=0)
    query = jnp.dot(source, operator, preferred_element_type=jnp.float32).astype(jnp.bfloat16)
    positive = jnp.sum(query.astype(jnp.float32) * target.astype(jnp.float32), axis=-1)
    scores = jnp.dot(query, negative.T, preferred_element_type=jnp.float32)
    slope = -jax.nn.sigmoid(-positive)
    neg_weight = (jax.nn.sigmoid(scores) * weight_neg).astype(jnp.bfloat16)
    query_grad = slope[:, None] * target.astype(jnp.float32) + jnp.dot(neg_weight, negative, preferred_element_type=jnp.float32)
    query_grad = query_grad.astype(jnp.bfloat16)
    target_grad = slope[:, None] * query.astype(jnp.float32)
    negative_grad = jnp.dot(neg_weight.T, query, preferred_element_type=jnp.float32)
    source_grad = jnp.dot(query_grad, operator.T, preferred_element_type=jnp.float32)
    operator_grad = jnp.dot(source.T, query_grad, preferred_element_type=jnp.float32)
    return source_grad, target_grad, negative_grad, operator_grad


def reference(entity_table, relation_ops, need_rows, send_offsets, source_ids, target_ids, negative_ids, relation_ids):
    devices = N_ROWS * N_REP
    need_list = need_rows.reshape(devices, N_ROWS, CAPACITY)
    offset_list = send_offsets.reshape(devices, N_ROWS + 1)
    source_list = source_ids.reshape(devices, BLOCKS, EDGES)
    target_list = target_ids.reshape(devices, BLOCKS, EDGES)
    negative_list = negative_ids.reshape(devices, BLOCKS, NEGATIVES)
    relation_list = relation_ids.reshape(devices, BLOCKS)
    owner_base = jnp.arange(N_ROWS, dtype=jnp.int32)[:, None] * ROWS_DEV
    weight_neg = NEGATIVES ** -0.5

    def per_device(carried, inputs):
        entity_acc, operator_acc = carried
        need_one, offsets, sources, targets, negatives, relations = inputs
        rows_global = (owner_base + need_one).reshape(-1).astype(jnp.int32)
        slots = jnp.take(entity_table, rows_global, axis=0)
        source_slot = locate(sources, offsets, CAPACITY)
        target_slot = locate(targets, offsets, CAPACITY)
        negative_slot = locate(negatives, offsets, CAPACITY)
        slot_grad = jnp.zeros((N_ROWS * CAPACITY, EMBED_DIM), jnp.float32)
        for block_index in range(BLOCKS):
            operator = relation_ops[relations[block_index]]
            source_grad, target_grad, negative_grad, operator_grad = block_terms(
                slots, operator, source_slot[block_index], target_slot[block_index], negative_slot[block_index], weight_neg)
            slot_grad = slot_grad.at[source_slot[block_index]].add(source_grad)
            slot_grad = slot_grad.at[target_slot[block_index]].add(target_grad)
            slot_grad = slot_grad.at[negative_slot[block_index]].add(negative_grad)
            operator_acc = operator_acc.at[relations[block_index]].add(operator_grad)
        entity_acc = entity_acc.at[rows_global].add(slot_grad)
        return (entity_acc, operator_acc), None

    initial = (jnp.zeros((ROWS_DEV * N_ROWS, EMBED_DIM), jnp.float32),
               jnp.zeros((RELATIONS, EMBED_DIM, EMBED_DIM), jnp.float32))
    (entity_acc, operator_acc), _ = lax.scan(
        per_device, initial, (need_list, offset_list, source_list, target_list, negative_list, relation_list))
    entity_grad = entity_acc.astype(jnp.bfloat16)
    relation_grad = operator_acc * (RELATIONS / (EDGES * BLOCKS * devices)) ** 0.5
    return entity_grad, relation_grad
```

```python
import functools

import jax
import jax.numpy as jnp
from jax import lax
from jax.experimental import pallas as pl
from jax.experimental.pallas import tpu as pltpu
from jax.sharding import PartitionSpec as P

LANES = 128
TILE = 8
REL_LANE = 16
CID_LANE = 64


def pack(rows):
    cubes = rows.reshape(rows.shape[0] // TILE, TILE, rows.shape[1])
    return jnp.concatenate([cubes[:, :, :LANES], cubes[:, :, LANES:]], axis=1).astype(jnp.bfloat16)


def unpack(packed):
    wide = packed.astype(jnp.float32)
    joined = jnp.concatenate([wide[:, :TILE, :], wide[:, TILE:, :]], axis=2)
    return joined.reshape(joined.shape[0] * TILE, joined.shape[2])


def column(messages, first_lane):
    count = messages.shape[0]
    wide = jnp.broadcast_to(messages.astype(jnp.float32), (count, TILE, LANES)).reshape(count * TILE, LANES)
    lane = lax.broadcasted_iota(jnp.int32, wide.shape, 1)
    row = lax.rem(lax.broadcasted_iota(jnp.int32, wide.shape, 0), TILE)
    return jnp.sum(jnp.where(lane == row + first_lane, wide, 0.0), axis=1, keepdims=True)


def dot(left, right, left_dim, right_dim):
    return lax.dot_general(
        left, right, (((left_dim,), (right_dim,)), ((), ())), preferred_element_type=jnp.float32
    )


def split(value):
    upper = value.astype(jnp.bfloat16)
    return upper, (value - upper.astype(jnp.float32)).astype(jnp.bfloat16)


def kernel(
    n_rows, n_rep, scale,
    relation_ref, head_ref, source_ref, target_ref, negative_ref, table_hbm, ops_hbm,
    entity_ref, relation_out,
    table, operators, requests, served, slots_in, grad_out, grad_in, op_out, op_in, relation_of, gathered,
    pair_count, negative_count, row_acc,
    local_sem, send_sem, receive_sem, gather_sem, fan_sem, pass_sem,
):
    devices = n_rows * n_rep
    my_row, my_rep = lax.axis_index("rows"), lax.axis_index("rep")
    me = my_row * n_rep + my_rep
    my_slot = my_rep * n_rows + my_row
    other_rep = n_rep - 1 - my_rep
    blocks = source_ref.shape[0]
    relations, width, _ = operators.shape
    reducers = width // TILE
    stride = devices // reducers
    weight_neg = negative_ref.shape[1] ** (-0.5)

    table_copy = pltpu.make_async_copy(table_hbm, table, local_sem.at[0])
    table_copy.start()
    ops_copy = pltpu.make_async_copy(ops_hbm, operators, local_sem.at[1])
    ops_copy.start()

    def remote(source, destination, send, receive, row, rep):
        return pltpu.make_async_remote_copy(
            src_ref=source, dst_ref=destination, send_sem=send, recv_sem=receive,
            device_id=(row, rep), device_id_type=pl.DeviceIdType.MESH,
        )

    def settle(buffer, semaphore):
        pltpu.make_async_copy(buffer, buffer, semaphore).wait()

    barrier = pltpu.get_barrier_semaphore()

    @pl.loop(1, devices)
    def _(step):
        other = lax.rem(me + step, devices)
        pl.semaphore_signal(
            barrier, inc=1, device_id=(lax.div(other, n_rep), lax.rem(other, n_rep)),
            device_id_type=pl.DeviceIdType.MESH,
        )

    pl.semaphore_wait(barrier, devices - 1)

    own_request = pltpu.make_async_copy(head_ref.at[my_row], requests.at[my_slot], receive_sem.at[0])
    own_request.start()

    @pl.loop(1, n_rows)
    def _(step):
        row = lax.rem(my_row + step, n_rows)
        remote(head_ref.at[row], requests.at[my_slot], send_sem.at[0], receive_sem.at[0], row, my_rep).start()

    @pl.loop(0, n_rows)
    def _(step):
        row = lax.rem(my_row + step, n_rows)
        remote(head_ref.at[row], requests.at[my_slot], send_sem.at[1], receive_sem.at[1], row, other_rep).start()

    compact = column(head_ref[...], CID_LANE).astype(jnp.int32)
    for block in range(blocks):
        hit = [
            (compact == ids[block : block + 1, :]).astype(jnp.float32).astype(jnp.bfloat16)
            for ids in (source_ref, target_ref, negative_ref)
        ]
        pair_count[block] = dot(hit[0], hit[1], 1, 1)
        ones = jnp.ones((TILE, hit[2].shape[1]), jnp.bfloat16)
        negative_count[block] = dot(ones, hit[2], 1, 1)

    settle(requests.at[pl.ds(my_rep * n_rows, n_rows)], receive_sem.at[0])
    wanted = column(requests[pl.ds(my_rep * n_rows, n_rows)], 0).astype(jnp.int32)
    table_copy.wait()
    step_rows = 512
    row_acc[...] = jnp.zeros_like(row_acc)

    @pl.loop(0, table.shape[0] // step_rows)
    def _(step):
        first = pl.multiple_of(step * step_rows, step_rows)
        lane = lax.broadcasted_iota(jnp.int32, (wanted.shape[0], step_rows), 1) + first
        pick = (wanted == lane).astype(jnp.float32).astype(jnp.bfloat16)
        row_acc[...] += dot(pick, table[pl.ds(first, step_rows), :], 1, 0)

    served[...] = pack(row_acc[...])
    own_rows = pltpu.make_async_copy(served.at[my_row], slots_in.at[my_row], receive_sem.at[2])
    own_rows.start()

    @pl.loop(1, n_rows)
    def _(step):
        row = lax.rem(my_row + step, n_rows)
        remote(served.at[row], slots_in.at[my_row], send_sem.at[2], receive_sem.at[2], row, my_rep).start()

    settle(requests.at[pl.ds(other_rep * n_rows, n_rows)], receive_sem.at[1])
    heads = requests[...].astype(jnp.float32)
    head_lane = lax.broadcasted_iota(jnp.int32, heads.shape, 2)
    for block in range(blocks):
        kind = jnp.sum(jnp.where(head_lane == REL_LANE + block, heads, 0.0), axis=2, keepdims=True)
        relation_of[block] = jnp.broadcast_to(kind, heads.shape)
    ops_copy.wait()
    settle(slots_in, receive_sem.at[2])

    slots = unpack(slots_in[...]).astype(jnp.bfloat16)
    slot_grad = jnp.zeros(slots.shape, jnp.float32)
    for block in range(blocks):
        operator = operators[relation_ref[block]]
        query = dot(slots, operator, 1, 0).astype(jnp.bfloat16)
        scores = dot(query, slots, 1, 1)
        pairs = pair_count[block]
        source_count = jnp.sum(pairs, axis=1, keepdims=True)
        coefficient = source_count * negative_count[block][:1, :] * (jax.nn.sigmoid(scores) * weight_neg)
        coefficient = coefficient - pairs * jax.nn.sigmoid(-scores)
        upper, lower = split(coefficient)
        query_grad = (dot(upper, slots, 1, 0) + dot(lower, slots, 1, 0)).astype(jnp.bfloat16)
        op_out[:, block] = pack(dot(slots, query_grad, 0, 0))
        slot_grad = slot_grad + dot(query_grad, operator, 1, 1)
        slot_grad = slot_grad + dot(upper, query, 0, 0) + dot(lower, query, 0, 0)
    grad_out[...] = pack(slot_grad)

    my_reducer = lax.div(me, stride)
    reducing = lax.rem(me, stride) == 0

    @pl.loop(0, reducers)
    def _(step):
        reducer = lax.rem(my_reducer + 1 + step, reducers)
        device = reducer * stride

        @pl.when(device != me)
        def _():
            remote(
                op_out.at[reducer], op_in.at[my_slot], send_sem.at[3], receive_sem.at[3],
                lax.div(device, n_rep), lax.rem(device, n_rep),
            ).start()

        @pl.when(device == me)
        def _():
            pltpu.make_async_copy(op_out.at[reducer], op_in.at[my_slot], receive_sem.at[3]).start()

    pltpu.make_async_copy(grad_out.at[my_row], grad_in.at[my_slot], receive_sem.at[4]).start()

    @pl.loop(1, devices)
    def _(step):
        device = lax.rem(me + step, devices)
        row = lax.div(device, n_rep)
        remote(
            grad_out.at[row], grad_in.at[my_slot], send_sem.at[4], receive_sem.at[4], row, lax.rem(device, n_rep)
        ).start()

    @pl.when(reducing)
    def _():
        settle(op_in, receive_sem.at[3])

        def add(source, totals):
            totals = list(totals)
            for block in range(blocks):
                term = op_in[source, block].astype(jnp.float32)
                kind = relation_of[block, source]
                for relation in range(relations):
                    totals[relation] = totals[relation] + jnp.where(kind == float(relation), term, 0.0)
            return tuple(totals)

        zero = jnp.zeros(op_in.shape[2:], jnp.float32)
        totals = lax.fori_loop(0, devices, add, (zero,) * relations)
        for relation in range(relations):
            gathered[my_reducer, relation] = (totals[relation] * scale).astype(jnp.bfloat16)

        piece = gathered.at[my_reducer]

        @pl.loop(1, n_rows)
        def _(step):
            row = lax.rem(my_row + step, n_rows)
            remote(piece, piece, fan_sem.at[row], gather_sem.at[my_reducer], row, my_rep).start()

        remote(piece, piece, fan_sem.at[my_row], gather_sem.at[my_reducer], my_row, other_rep).start()

    settle(grad_in, receive_sem.at[4])
    all_rows = column(requests[...], 0).astype(jnp.int32)
    grads = unpack(grad_in[...]).astype(jnp.bfloat16)
    half = entity_ref.shape[0]

    @pl.loop(0, half // step_rows)
    def _(step):
        first = pl.multiple_of(step * step_rows, step_rows)
        lane = lax.broadcasted_iota(jnp.int32, (all_rows.shape[0], step_rows), 1) + first + my_rep * half
        place = (all_rows == lane).astype(jnp.float32).astype(jnp.bfloat16)
        entity_ref[pl.ds(first, step_rows), :] = dot(place, grads, 0, 0).astype(jnp.bfloat16)

    def spread(reducer):
        rows = gathered[reducer].astype(jnp.float32)
        first = pl.multiple_of(reducer * TILE, TILE)
        relation_out[:, pl.ds(first, TILE), :] = jnp.concatenate([rows[:, :TILE, :], rows[:, TILE:, :]], axis=2)

    @pl.loop(0, reducers)
    def _(step):
        reducer = lax.rem(my_reducer + reducers - step, reducers)
        device = reducer * stride
        piece = gathered.at[reducer]

        @pl.when(lax.rem(device, n_rep) == my_rep)
        def _():
            @pl.when(device != me)
            def _():
                settle(piece, gather_sem.at[reducer])
                remote(piece, piece, pass_sem.at[reducer], gather_sem.at[reducer], my_row, other_rep).start()

            spread(reducer)

    @pl.loop(0, reducers)
    def _(step):
        reducer = lax.rem(my_reducer + reducers - step, reducers)

        @pl.when(lax.rem(reducer * stride, n_rep) != my_rep)
        def _():
            settle(gathered.at[reducer], gather_sem.at[reducer])
            spread(reducer)

    settle(head_ref.at[pl.ds(0, n_rows - 1)], send_sem.at[0])
    settle(head_ref, send_sem.at[1])
    settle(served.at[pl.ds(0, n_rows - 1)], send_sem.at[2])
    settle(op_out.at[pl.ds(0, reducers - 1)], send_sem.at[3])

    @pl.when(jnp.logical_not(reducing))
    def _():
        settle(op_out.at[0], send_sem.at[3])

    settle(grad_in.at[pl.ds(0, devices - 1)], send_sem.at[4])

    @pl.when(reducing)
    def _():
        @pl.loop(0, n_rows)
        def _(row):
            settle(gathered.at[my_reducer], fan_sem.at[row])

    @pl.loop(0, reducers)
    def _(reducer):
        device = reducer * stride

        @pl.when(jnp.logical_and(lax.rem(device, n_rep) == my_rep, device != me))
        def _():
            settle(gathered.at[reducer], pass_sem.at[reducer])


def shards(
    entity_table, relation_ops, need_rows, send_offsets, source_ids, target_ids, negative_ids, relation_ids
):
    n_rows, n_rep = lax.axis_size("rows"), lax.axis_size("rep")
    devices = n_rows * n_rep
    need = need_rows[0, 0]
    capacity = need.shape[1]
    offsets = send_offsets[0, 0]
    blocks, edges = source_ids.shape[2:]
    relations, width, _ = relation_ops.shape
    reducers = width // TILE
    slot_lane = jnp.arange(capacity, dtype=jnp.int32)[None, :]
    compact = offsets[:-1, None] + slot_lane
    compact = jnp.where(compact < offsets[1:, None], compact, -1)
    kinds = jnp.broadcast_to(relation_ids[0, 0][None, :], (n_rows, blocks))
    head = (
        jnp.pad(need, ((0, 0), (0, LANES - capacity)))
        + jnp.pad(kinds, ((0, 0), (REL_LANE, LANES - REL_LANE - blocks)))
        + jnp.pad(compact, ((0, 0), (CID_LANE, LANES - CID_LANE - capacity)))
    ).reshape(n_rows, 1, LANES)
    scale = (relations / (edges * blocks * devices)) ** 0.5
    packed = (2 * TILE, LANES)
    slots = n_rows * capacity
    vmem = pl.BlockSpec(memory_space=pltpu.VMEM)
    anywhere = pl.BlockSpec(memory_space=pl.ANY)
    return pl.pallas_call(
        functools.partial(kernel, n_rows, n_rep, scale),
        out_shape=(
            jax.ShapeDtypeStruct((entity_table.shape[0] // n_rep, width), jnp.bfloat16),
            jax.ShapeDtypeStruct(relation_ops.shape, jnp.float32),
        ),
        in_specs=[pl.BlockSpec(memory_space=pltpu.SMEM), vmem, vmem, vmem, vmem, anywhere, anywhere],
        out_specs=(vmem, vmem),
        scratch_shapes=[
            pltpu.VMEM(entity_table.shape, jnp.bfloat16),
            pltpu.VMEM(relation_ops.shape, jnp.bfloat16),
            pltpu.VMEM((devices, 1, LANES), jnp.int32),
            pltpu.VMEM((n_rows, *packed), jnp.bfloat16),
            pltpu.VMEM((n_rows, *packed), jnp.bfloat16),
            pltpu.VMEM((n_rows, *packed), jnp.bfloat16),
            pltpu.VMEM((devices, *packed), jnp.bfloat16),
            pltpu.VMEM((reducers, blocks, *packed), jnp.bfloat16),
            pltpu.VMEM((devices, blocks, *packed), jnp.bfloat16),
            pltpu.VMEM((blocks, devices, 1, LANES), jnp.float32),
            pltpu.VMEM((reducers, relations, *packed), jnp.bfloat16),
            pltpu.VMEM((blocks, slots, slots), jnp.float32),
            pltpu.VMEM((blocks, TILE, slots), jnp.float32),
            pltpu.VMEM((slots, width), jnp.float32),
            pltpu.SemaphoreType.DMA((2,)),
            pltpu.SemaphoreType.DMA((5,)),
            pltpu.SemaphoreType.DMA((5,)),
            pltpu.SemaphoreType.DMA((reducers,)),
            pltpu.SemaphoreType.DMA((n_rows,)),
            pltpu.SemaphoreType.DMA((reducers,)),
        ],
        compiler_params=pltpu.CompilerParams(
            collective_id=0, has_side_effects=True, vmem_limit_bytes=52 * 1024 * 1024
        ),
    )(
        relation_ids[0, 0], head, source_ids[0, 0], target_ids[0, 0], negative_ids[0, 0],
        entity_table, relation_ops,
    )


def solution(mesh):
    return jax.shard_map(
        shards,
        mesh=mesh,
        in_specs=(
            P("rows", None),
            P(),
            P("rows", "rep", None, None),
            P("rows", "rep", None),
            P("rows", "rep", None, None),
            P("rows", "rep", None, None),
            P("rows", "rep", None, None),
            P("rows", "rep", None),
        ),
        out_specs=(P(("rows", "rep"), None), P()),
        check_vma=False,
    )
```

```python
import functools

import jax
import jax.numpy as jnp
from jax import lax
from jax.experimental import pallas as pl
from jax.experimental.pallas import tpu as pltpu
from jax.sharding import PartitionSpec as P

LANES = 128
TILE = 8
REL_LANE = 16
PLANE = 4


def pack(rows):
    cubes = rows.reshape(rows.shape[0] // TILE, TILE, rows.shape[1])
    return jnp.concatenate([cubes[:, :, :LANES], cubes[:, :, LANES:]], axis=1).astype(jnp.bfloat16)


def unpack(packed):
    wide = packed.astype(jnp.float32)
    joined = jnp.concatenate([wide[:, :TILE, :], wide[:, TILE:, :]], axis=2)
    return joined.reshape(joined.shape[0] * TILE, joined.shape[2])


def column(messages, first_lane):
    count = messages.shape[0]
    wide = jnp.broadcast_to(messages.astype(jnp.float32), (count, TILE, LANES)).reshape(count * TILE, LANES)
    lane = lax.broadcasted_iota(jnp.int32, wide.shape, 1)
    row = lax.rem(lax.broadcasted_iota(jnp.int32, wide.shape, 0), TILE)
    return jnp.sum(jnp.where(lane == row + first_lane, wide, 0.0), axis=1, keepdims=True)


def dot(left, right, left_dim, right_dim):
    return lax.dot_general(
        left, right, (((left_dim,), (right_dim,)), ((), ())), preferred_element_type=jnp.float32
    )


def split(value):
    upper = value.astype(jnp.bfloat16)
    return upper, (value - upper.astype(jnp.float32)).astype(jnp.bfloat16)


def kernel(
    n_rows, n_rep, scale,
    relation_ref, offset_ref, need_hbm, source_hbm, target_hbm, negative_hbm, table_hbm, ops_hbm,
    entity_hbm, relation_out,
    need_ref, source_ref, target_ref, negative_ref, head_ref, compact_ref, entity_ref,
    table, operators, requests, served, slots_in, grad_out, grad_in, op_out, op_in, relation_of, gathered,
    pair_count, negative_count, row_acc,
    local_sem, send_sem, receive_sem, gather_sem, fan_sem, pass_sem,
):
    devices = n_rows * n_rep
    my_row, my_rep = lax.axis_index("rows"), lax.axis_index("rep")
    me = my_row * n_rep + my_rep
    my_slot = my_rep * n_rows + my_row
    other_rep = n_rep - 1 - my_rep
    blocks = source_ref.shape[0]
    relations, width, _ = operators.shape
    reducers = width // TILE
    stride = devices // reducers
    weight_neg = negative_ref.shape[1] ** (-0.5)

    table_copy = pltpu.make_async_copy(table_hbm, table, local_sem.at[0])
    table_copy.start()
    ops_copy = pltpu.make_async_copy(ops_hbm, operators, local_sem.at[1])
    ops_copy.start()
    need_copy = pltpu.make_async_copy(need_hbm, need_ref, local_sem.at[2])
    need_copy.start()
    id_copies = [
        pltpu.make_async_copy(hbm, ref, local_sem.at[3 + index])
        for index, (hbm, ref) in enumerate(
            ((source_hbm, source_ref), (target_hbm, target_ref), (negative_hbm, negative_ref))
        )
    ]
    for id_copy in id_copies:
        id_copy.start()

    def remote(source, destination, send, receive, row, rep):
        return pltpu.make_async_remote_copy(
            src_ref=source, dst_ref=destination, send_sem=send, recv_sem=receive,
            device_id=(row, rep), device_id_type=pl.DeviceIdType.MESH,
        )

    def settle(buffer, semaphore):
        pltpu.make_async_copy(buffer, buffer, semaphore).wait()

    barrier = pltpu.get_barrier_semaphore()

    @pl.loop(1, devices)
    def _(step):
        other = lax.rem(me + step, devices)
        pl.semaphore_signal(
            barrier, inc=1, device_id=(lax.div(other, n_rep), lax.rem(other, n_rep)),
            device_id_type=pl.DeviceIdType.MESH,
        )

    lane = lax.broadcasted_iota(jnp.int32, (TILE, LANES), 1)
    sublane = lax.broadcasted_iota(jnp.int32, (TILE, LANES), 0)
    kinds = jnp.zeros((1, LANES), jnp.int32)
    for block in range(blocks):
        kinds = jnp.where(lane[:1] == REL_LANE + block, relation_ref[block], kinds)
    need_copy.wait()
    need = need_ref[...].astype(jnp.float32)
    for row in range(n_rows):
        wide = jnp.where(lane == sublane, jnp.broadcast_to(need[:, row : row + 1], lane.shape), 0.0)
        head_ref[row] = jnp.sum(wide, axis=0, keepdims=True).astype(jnp.int32) + kinds
        first_id = offset_ref[row]
        slot_id = first_id + sublane
        compact_ref[row * TILE : (row + 1) * TILE, :] = jnp.where(slot_id < offset_ref[row + 1], slot_id, -1)

    pl.semaphore_wait(barrier, devices - 1)

    own_request = pltpu.make_async_copy(head_ref.at[my_row], requests.at[my_slot], receive_sem.at[0])
    own_request.start()

    @pl.loop(1, n_rows)
    def _(step):
        row = lax.rem(my_row + step, n_rows)
        remote(head_ref.at[row], requests.at[my_slot], send_sem.at[0], receive_sem.at[0], row, my_rep).start()

    @pl.loop(0, n_rows)
    def _(step):
        row = lax.rem(my_row + step, n_rows)
        remote(head_ref.at[row], requests.at[my_slot], send_sem.at[1], receive_sem.at[1], row, other_rep).start()

    for id_copy in id_copies:
        id_copy.wait()
    compact = compact_ref[:, :1]
    for block in range(blocks):
        hit = [
            (compact == ids[block : block + 1, :]).astype(jnp.float32).astype(jnp.bfloat16)
            for ids in (source_ref, target_ref, negative_ref)
        ]
        pair_count[block] = dot(hit[0], hit[1], 1, 1)
        ones = jnp.ones((TILE, hit[2].shape[1]), jnp.bfloat16)
        negative_count[block] = dot(ones, hit[2], 1, 1)

    settle(requests.at[pl.ds(my_rep * n_rows, n_rows)], receive_sem.at[0])
    wanted = column(requests[pl.ds(my_rep * n_rows, n_rows)], 0).astype(jnp.int32)
    table_copy.wait()
    step_rows = 512
    row_acc[...] = jnp.zeros_like(row_acc)

    @pl.loop(0, table.shape[0] // step_rows)
    def _(step):
        first = pl.multiple_of(step * step_rows, step_rows)
        lane = lax.broadcasted_iota(jnp.int32, (wanted.shape[0], step_rows), 1) + first
        pick = (wanted == lane).astype(jnp.float32).astype(jnp.bfloat16)
        row_acc[...] += dot(pick, table[pl.ds(first, step_rows), :], 1, 0)

    served[...] = pack(row_acc[...])
    own_rows = pltpu.make_async_copy(served.at[my_row], slots_in.at[my_row], receive_sem.at[2])
    own_rows.start()

    @pl.loop(1, n_rows)
    def _(step):
        row = lax.rem(my_row + step, n_rows)
        remote(served.at[row], slots_in.at[my_row], send_sem.at[2], receive_sem.at[2], row, my_rep).start()

    settle(requests.at[pl.ds(other_rep * n_rows, n_rows)], receive_sem.at[1])
    heads = requests[...].astype(jnp.float32)
    head_lane = lax.broadcasted_iota(jnp.int32, heads.shape, 2)
    for block in range(blocks):
        kind = jnp.sum(jnp.where(head_lane == REL_LANE + block, heads, 0.0), axis=2, keepdims=True)
        relation_of[block] = jnp.broadcast_to(kind, heads.shape)
    ops_copy.wait()
    settle(slots_in, receive_sem.at[2])

    slots = unpack(slots_in[...]).astype(jnp.bfloat16)
    slot_grad = jnp.zeros(slots.shape, jnp.float32)
    for block in range(blocks):
        operator = operators[relation_ref[block]]
        query = dot(slots, operator, 1, 0).astype(jnp.bfloat16)
        scores = dot(query, slots, 1, 1)
        pairs = pair_count[block]
        source_count = jnp.sum(pairs, axis=1, keepdims=True)
        coefficient = source_count * negative_count[block][:1, :] * (jax.nn.sigmoid(scores) * weight_neg)
        coefficient = coefficient - pairs * jax.nn.sigmoid(-scores)
        upper, lower = split(coefficient)
        query_grad = (dot(upper, slots, 1, 0) + dot(lower, slots, 1, 0)).astype(jnp.bfloat16)
        op_out[:, block] = pack(dot(slots, query_grad, 0, 0))
        slot_grad = slot_grad + dot(query_grad, operator, 1, 1)
        slot_grad = slot_grad + dot(upper, query, 0, 0) + dot(lower, query, 0, 0)
    grad_out[...] = pack(slot_grad)

    my_reducer = lax.div(me, stride)
    reducing = lax.rem(me, stride) == 0

    @pl.loop(0, reducers)
    def _(step):
        reducer = lax.rem(my_reducer + 1 + step, reducers)
        device = reducer * stride

        @pl.when(device != me)
        def _():
            remote(
                op_out.at[reducer], op_in.at[my_slot], send_sem.at[3], receive_sem.at[3],
                lax.div(device, n_rep), lax.rem(device, n_rep),
            ).start()

        @pl.when(device == me)
        def _():
            pltpu.make_async_copy(op_out.at[reducer], op_in.at[my_slot], receive_sem.at[3]).start()

    pltpu.make_async_copy(grad_out.at[my_row], grad_in.at[my_slot], receive_sem.at[4]).start()

    @pl.loop(1, devices)
    def _(step):
        device = lax.rem(me + step, devices)
        row = lax.div(device, n_rep)
        remote(
            grad_out.at[row], grad_in.at[my_slot], send_sem.at[4], receive_sem.at[4], row, lax.rem(device, n_rep)
        ).start()

    @pl.when(reducing)
    def _():
        settle(op_in, receive_sem.at[3])

        def add(source, totals):
            totals = list(totals)
            for block in range(blocks):
                term = op_in[source, block].astype(jnp.float32)
                kind = relation_of[block, source]
                for relation in range(relations):
                    totals[relation] = totals[relation] + jnp.where(kind == float(relation), term, 0.0)
            return tuple(totals)

        zero = jnp.zeros(op_in.shape[2:], jnp.float32)
        totals = lax.fori_loop(0, devices, add, (zero,) * relations)
        for relation in range(relations):
            gathered[my_reducer, relation] = (totals[relation] * scale).astype(jnp.bfloat16)

        piece = gathered.at[my_reducer]

        @pl.loop(1, n_rows // PLANE)
        def _(step):
            row = lax.rem(my_row + step * PLANE, n_rows)
            remote(piece, piece, fan_sem.at[PLANE + step], gather_sem.at[my_reducer], row, my_rep).start()

        for step in range(1, PLANE):
            row = lax.div(my_row, PLANE) * PLANE + lax.rem(my_row + step, PLANE)
            remote(piece, piece, fan_sem.at[step], gather_sem.at[my_reducer], row, my_rep).start()

        remote(piece, piece, fan_sem.at[0], gather_sem.at[my_reducer], my_row, other_rep).start()

    settle(grad_in, receive_sem.at[4])
    all_rows = column(requests[...], 0).astype(jnp.int32)
    grads = unpack(grad_in[...]).astype(jnp.bfloat16)
    half = entity_ref.shape[0]

    @pl.loop(0, half // step_rows)
    def _(step):
        first = pl.multiple_of(step * step_rows, step_rows)
        lane = lax.broadcasted_iota(jnp.int32, (all_rows.shape[0], step_rows), 1) + first + my_rep * half
        place = (all_rows == lane).astype(jnp.float32).astype(jnp.bfloat16)
        entity_ref[pl.ds(first, step_rows), :] = dot(place, grads, 0, 0).astype(jnp.bfloat16)

    entity_copy = pltpu.make_async_copy(entity_ref, entity_hbm, local_sem.at[6])
    entity_copy.start()

    def mine(reducer):
        device = reducer * stride
        same_rep = lax.rem(device, n_rep) == my_rep
        same_column = lax.rem(lax.div(device, n_rep), PLANE) == lax.rem(my_row, PLANE)
        first = jnp.logical_and(jnp.logical_and(same_rep, same_column), device != me)
        second = jnp.logical_and(same_rep, jnp.logical_not(same_column))
        return first, second

    @pl.loop(0, reducers)
    def _(step):
        reducer = lax.rem(my_reducer + 1 + step, reducers)
        piece = gathered.at[reducer]

        @pl.when(mine(reducer)[0])
        def _():
            settle(piece, gather_sem.at[reducer])
            for hop in range(1, PLANE):
                row = lax.div(my_row, PLANE) * PLANE + lax.rem(my_row + hop, PLANE)
                remote(piece, piece, pass_sem.at[reducer, hop], gather_sem.at[reducer], row, my_rep).start()
            remote(piece, piece, pass_sem.at[reducer, 0], gather_sem.at[reducer], my_row, other_rep).start()

    @pl.loop(0, reducers)
    def _(step):
        reducer = lax.rem(my_reducer + 1 + step, reducers)
        piece = gathered.at[reducer]

        @pl.when(mine(reducer)[1])
        def _():
            settle(piece, gather_sem.at[reducer])
            remote(piece, piece, pass_sem.at[reducer, 0], gather_sem.at[reducer], my_row, other_rep).start()

    @pl.loop(0, reducers // 2)
    def _(pair):
        halves = []
        for reducer in (2 * pair, 2 * pair + 1):

            @pl.when(lax.rem(reducer * stride, n_rep) != my_rep)
            def _():
                settle(gathered.at[reducer], gather_sem.at[reducer])

            rows = gathered[reducer].astype(jnp.float32)
            halves.append(jnp.concatenate([rows[:, :TILE, :], rows[:, TILE:, :]], axis=2))
        first = pl.multiple_of(pair * 2 * TILE, 2 * TILE)
        relation_out[:, pl.ds(first, 2 * TILE), :] = jnp.concatenate(halves, axis=1).astype(jnp.bfloat16)

    settle(head_ref.at[pl.ds(0, n_rows - 1)], send_sem.at[0])
    settle(head_ref, send_sem.at[1])
    settle(served.at[pl.ds(0, n_rows - 1)], send_sem.at[2])
    settle(op_out.at[pl.ds(0, reducers - 1)], send_sem.at[3])

    @pl.when(jnp.logical_not(reducing))
    def _():
        settle(op_out.at[0], send_sem.at[3])

    settle(grad_in.at[pl.ds(0, devices - 1)], send_sem.at[4])

    @pl.when(reducing)
    def _():
        for step in range(PLANE):
            settle(gathered.at[my_reducer], fan_sem.at[step])

        @pl.loop(1, n_rows // PLANE)
        def _(step):
            settle(gathered.at[my_reducer], fan_sem.at[PLANE + step])

    @pl.loop(0, reducers)
    def _(reducer):
        first, second = mine(reducer)

        @pl.when(jnp.logical_or(first, second))
        def _():
            settle(gathered.at[reducer], pass_sem.at[reducer, 0])

        @pl.when(first)
        def _():
            for hop in range(1, PLANE):
                settle(gathered.at[reducer], pass_sem.at[reducer, hop])

    entity_copy.wait()


def shards(
    entity_table, relation_ops, need_rows, send_offsets, source_ids, target_ids, negative_ids, relation_ids
):
    n_rows, n_rep = lax.axis_size("rows"), lax.axis_size("rep")
    devices = n_rows * n_rep
    need = need_rows[0, 0]
    capacity = need.shape[1]
    blocks, edges = source_ids.shape[2:]
    relations, width, _ = relation_ops.shape
    reducers = width // TILE
    scale = (relations / (edges * blocks * devices)) ** 0.5
    packed = (2 * TILE, LANES)
    slots = n_rows * capacity
    hbm = pl.BlockSpec(memory_space=pltpu.HBM)
    smem = pl.BlockSpec(memory_space=pltpu.SMEM)
    entity_shape = (entity_table.shape[0] // n_rep, width)
    entity_grad, relation_grad = pl.pallas_call(
        functools.partial(kernel, n_rows, n_rep, scale),
        out_shape=(
            jax.ShapeDtypeStruct(entity_shape, jnp.bfloat16),
            jax.ShapeDtypeStruct(relation_ops.shape, jnp.bfloat16),
        ),
        in_specs=[smem, smem] + [hbm] * 6,
        out_specs=(hbm, pl.BlockSpec(memory_space=pltpu.VMEM)),
        scratch_shapes=[
            pltpu.VMEM((capacity, n_rows), jnp.int32),
            pltpu.VMEM((blocks, edges), jnp.int32),
            pltpu.VMEM((blocks, edges), jnp.int32),
            pltpu.VMEM((blocks, negative_ids.shape[-1]), jnp.int32),
            pltpu.VMEM((n_rows, 1, LANES), jnp.int32),
            pltpu.VMEM((slots, LANES), jnp.int32),
            pltpu.VMEM(entity_shape, jnp.bfloat16),
            pltpu.VMEM(entity_table.shape, jnp.bfloat16),
            pltpu.VMEM(relation_ops.shape, jnp.bfloat16),
            pltpu.VMEM((devices, 1, LANES), jnp.int32),
            pltpu.VMEM((n_rows, *packed), jnp.bfloat16),
            pltpu.VMEM((n_rows, *packed), jnp.bfloat16),
            pltpu.VMEM((n_rows, *packed), jnp.bfloat16),
            pltpu.VMEM((devices, *packed), jnp.bfloat16),
            pltpu.VMEM((reducers, blocks, *packed), jnp.bfloat16),
            pltpu.VMEM((devices, blocks, *packed), jnp.bfloat16),
            pltpu.VMEM((blocks, devices, 1, LANES), jnp.float32),
            pltpu.VMEM((reducers, relations, *packed), jnp.bfloat16),
            pltpu.VMEM((blocks, slots, slots), jnp.float32),
            pltpu.VMEM((blocks, TILE, slots), jnp.float32),
            pltpu.VMEM((slots, width), jnp.float32),
            pltpu.SemaphoreType.DMA((7,)),
            pltpu.SemaphoreType.DMA((5,)),
            pltpu.SemaphoreType.DMA((5,)),
            pltpu.SemaphoreType.DMA((reducers,)),
            pltpu.SemaphoreType.DMA((PLANE + n_rows // PLANE,)),
            pltpu.SemaphoreType.DMA((reducers, PLANE)),
        ],
        compiler_params=pltpu.CompilerParams(
            collective_id=0, has_side_effects=True, vmem_limit_bytes=64 * 1024 * 1024 - 16384
        ),
    )(
        relation_ids[0, 0], send_offsets[0, 0], need.T, source_ids[0, 0], target_ids[0, 0], negative_ids[0, 0],
        entity_table, relation_ops,
    )
    return entity_grad, relation_grad.astype(jnp.float32)


def solution(mesh):
    return jax.shard_map(
        shards,
        mesh=mesh,
        in_specs=(
            P("rows", None),
            P(),
            P("rows", "rep", None, None),
            P("rows", "rep", None),
            P("rows", "rep", None, None),
            P("rows", "rep", None, None),
            P("rows", "rep", None, None),
            P("rows", "rep", None),
        ),
        out_specs=(P(("rows", "rep"), None), P()),
        check_vma=False,
    )
```

```python
import functools

import jax
import jax.numpy as jnp
from jax import lax
from jax.experimental import pallas as pl
from jax.experimental.pallas import tpu as pltpu
from jax.sharding import PartitionSpec as P

LANES = 128
TILE = 8
REL_LANE = 16
PLANE = 4


def pack(rows):
    cubes = rows.reshape(rows.shape[0] // TILE, TILE, rows.shape[1])
    return jnp.concatenate([cubes[:, :, :LANES], cubes[:, :, LANES:]], axis=1).astype(jnp.bfloat16)


def unpack(packed):
    wide = packed.astype(jnp.float32)
    joined = jnp.concatenate([wide[:, :TILE, :], wide[:, TILE:, :]], axis=2)
    return joined.reshape(joined.shape[0] * TILE, joined.shape[2])


def column(messages, first_lane):
    count = messages.shape[0]
    wide = jnp.broadcast_to(messages.astype(jnp.float32), (count, TILE, LANES)).reshape(count * TILE, LANES)
    lane = lax.broadcasted_iota(jnp.int32, wide.shape, 1)
    row = lax.rem(lax.broadcasted_iota(jnp.int32, wide.shape, 0), TILE)
    return jnp.sum(jnp.where(lane == row + first_lane, wide, 0.0), axis=1, keepdims=True)


def dot(left, right, left_dim, right_dim):
    return lax.dot_general(
        left, right, (((left_dim,), (right_dim,)), ((), ())), preferred_element_type=jnp.float32
    )


def split(value):
    upper = value.astype(jnp.bfloat16)
    return upper, (value - upper.astype(jnp.float32)).astype(jnp.bfloat16)


def kernel(
    n_rows, n_rep, scale,
    relation_ref, offset_ref, need_hbm, source_hbm, target_hbm, negative_hbm, table_hbm, ops_hbm,
    entity_hbm, relation_out,
    need_ref, source_ref, target_ref, negative_ref, head_ref, compact_ref, entity_ref,
    table, operators, requests, served, slots_in, grad_out, grad_in, op_out, op_in, relation_of, gathered,
    pair_count, negative_count, row_acc,
    local_sem, send_sem, receive_sem, gather_sem, fan_sem, pass_sem,
):
    devices = n_rows * n_rep
    my_row, my_rep = lax.axis_index("rows"), lax.axis_index("rep")
    me = my_row * n_rep + my_rep
    my_slot = my_rep * n_rows + my_row
    other_rep = n_rep - 1 - my_rep
    blocks = source_ref.shape[0]
    relations, width, _ = operators.shape
    reducers = width // TILE
    stride = devices // reducers
    weight_neg = negative_ref.shape[1] ** (-0.5)

    table_copy = pltpu.make_async_copy(table_hbm, table, local_sem.at[0])
    table_copy.start()
    ops_copy = pltpu.make_async_copy(ops_hbm, operators, local_sem.at[1])
    ops_copy.start()
    need_copy = pltpu.make_async_copy(need_hbm, need_ref, local_sem.at[2])
    need_copy.start()
    id_copies = [
        pltpu.make_async_copy(hbm, ref, local_sem.at[3 + index])
        for index, (hbm, ref) in enumerate(
            ((source_hbm, source_ref), (target_hbm, target_ref), (negative_hbm, negative_ref))
        )
    ]
    for id_copy in id_copies:
        id_copy.start()

    def remote(source, destination, send, receive, row, rep):
        return pltpu.make_async_remote_copy(
            src_ref=source, dst_ref=destination, send_sem=send, recv_sem=receive,
            device_id=(row, rep), device_id_type=pl.DeviceIdType.MESH,
        )

    def settle(buffer, semaphore):
        pltpu.make_async_copy(buffer, buffer, semaphore).wait()

    barrier = pltpu.get_barrier_semaphore()

    @pl.loop(1, devices)
    def _(step):
        other = lax.rem(me + step, devices)
        pl.semaphore_signal(
            barrier, inc=1, device_id=(lax.div(other, n_rep), lax.rem(other, n_rep)),
            device_id_type=pl.DeviceIdType.MESH,
        )

    lane = lax.broadcasted_iota(jnp.int32, (TILE, LANES), 1)
    sublane = lax.broadcasted_iota(jnp.int32, (TILE, LANES), 0)
    kinds = jnp.zeros((1, LANES), jnp.int32)
    for block in range(blocks):
        kinds = jnp.where(lane[:1] == REL_LANE + block, relation_ref[block], kinds)
    need_copy.wait()
    need = need_ref[...].astype(jnp.float32)
    for row in range(n_rows):
        wide = jnp.where(lane == sublane, jnp.broadcast_to(need[:, row : row + 1], lane.shape), 0.0)
        head_ref[row] = jnp.sum(wide, axis=0, keepdims=True).astype(jnp.int32) + kinds
        first_id = offset_ref[row]
        slot_id = first_id + sublane
        compact_ref[row * TILE : (row + 1) * TILE, :] = jnp.where(slot_id < offset_ref[row + 1], slot_id, -1)

    pl.semaphore_wait(barrier, devices - 1)

    own_request = pltpu.make_async_copy(head_ref.at[my_row], requests.at[my_slot], receive_sem.at[0])
    own_request.start()

    @pl.loop(1, n_rows)
    def _(step):
        row = lax.rem(my_row + step, n_rows)
        remote(head_ref.at[row], requests.at[my_slot], send_sem.at[0], receive_sem.at[0], row, my_rep).start()

    @pl.loop(0, n_rows)
    def _(step):
        row = lax.rem(my_row + step, n_rows)
        remote(head_ref.at[row], requests.at[my_slot], send_sem.at[1], receive_sem.at[1], row, other_rep).start()

    for id_copy in id_copies:
        id_copy.wait()
    compact = compact_ref[:, :1]
    for block in range(blocks):
        hit = [
            (compact == ids[block : block + 1, :]).astype(jnp.float32).astype(jnp.bfloat16)
            for ids in (source_ref, target_ref, negative_ref)
        ]
        pair_count[block] = dot(hit[0], hit[1], 1, 1)
        ones = jnp.ones((TILE, hit[2].shape[1]), jnp.bfloat16)
        negative_count[block] = dot(ones, hit[2], 1, 1)

    settle(requests.at[pl.ds(my_rep * n_rows, n_rows)], receive_sem.at[0])
    wanted = column(requests[pl.ds(my_rep * n_rows, n_rows)], 0).astype(jnp.int32)
    table_copy.wait()
    step_rows = 512
    row_acc[...] = jnp.zeros_like(row_acc)

    @pl.loop(0, table.shape[0] // step_rows, unroll=4)
    def _(step):
        first = pl.multiple_of(step * step_rows, step_rows)
        lane = lax.broadcasted_iota(jnp.int32, (wanted.shape[0], step_rows), 1) + first
        pick = (wanted == lane).astype(jnp.float32).astype(jnp.bfloat16)
        row_acc[...] += dot(pick, table[pl.ds(first, step_rows), :], 1, 0)

    served[...] = pack(row_acc[...])
    own_rows = pltpu.make_async_copy(served.at[my_row], slots_in.at[my_row], receive_sem.at[2])
    own_rows.start()

    @pl.loop(1, n_rows)
    def _(step):
        row = lax.rem(my_row + step, n_rows)
        remote(served.at[row], slots_in.at[my_row], send_sem.at[2], receive_sem.at[2], row, my_rep).start()

    settle(requests.at[pl.ds(other_rep * n_rows, n_rows)], receive_sem.at[1])
    heads = requests[...].astype(jnp.float32)
    head_lane = lax.broadcasted_iota(jnp.int32, heads.shape, 2)
    for block in range(blocks):
        kind = jnp.sum(jnp.where(head_lane == REL_LANE + block, heads, 0.0), axis=2, keepdims=True)
        relation_of[block] = jnp.broadcast_to(kind, heads.shape)
    ops_copy.wait()
    settle(slots_in, receive_sem.at[2])

    slots = unpack(slots_in[...]).astype(jnp.bfloat16)
    slot_grad = jnp.zeros(slots.shape, jnp.float32)
    for block in range(blocks):
        operator = operators[relation_ref[block]]
        query = dot(slots, operator, 1, 0).astype(jnp.bfloat16)
        scores = dot(query, slots, 1, 1)
        pairs = pair_count[block]
        source_count = jnp.sum(pairs, axis=1, keepdims=True)
        coefficient = source_count * negative_count[block][:1, :] * (jax.nn.sigmoid(scores) * weight_neg)
        coefficient = coefficient - pairs * jax.nn.sigmoid(-scores)
        upper, lower = split(coefficient)
        query_grad = (dot(upper, slots, 1, 0) + dot(lower, slots, 1, 0)).astype(jnp.bfloat16)
        op_out[:, block] = pack(dot(slots, query_grad, 0, 0))
        slot_grad = slot_grad + dot(query_grad, operator, 1, 1)
        slot_grad = slot_grad + dot(upper, query, 0, 0) + dot(lower, query, 0, 0)
    grad_out[...] = pack(slot_grad)

    my_reducer = lax.div(me, stride)
    reducing = lax.rem(me, stride) == 0

    @pl.loop(0, reducers)
    def _(step):
        reducer = lax.rem(my_reducer + 1 + step, reducers)
        device = reducer * stride

        @pl.when(device != me)
        def _():
            remote(
                op_out.at[reducer], op_in.at[my_slot], send_sem.at[3], receive_sem.at[3],
                lax.div(device, n_rep), lax.rem(device, n_rep),
            ).start()

        @pl.when(device == me)
        def _():
            pltpu.make_async_copy(op_out.at[reducer], op_in.at[my_slot], receive_sem.at[3]).start()

    pltpu.make_async_copy(grad_out.at[my_row], grad_in.at[my_slot], receive_sem.at[4]).start()

    @pl.loop(1, devices)
    def _(step):
        device = lax.rem(me + step, devices)
        row = lax.div(device, n_rep)
        remote(
            grad_out.at[row], grad_in.at[my_slot], send_sem.at[4], receive_sem.at[4], row, lax.rem(device, n_rep)
        ).start()

    @pl.when(reducing)
    def _():
        settle(op_in, receive_sem.at[3])

        def add(source, totals):
            totals = list(totals)
            for block in range(blocks):
                term = op_in[source, block].astype(jnp.float32)
                kind = relation_of[block, source]
                for relation in range(relations):
                    totals[relation] = totals[relation] + jnp.where(kind == float(relation), term, 0.0)
            return tuple(totals)

        zero = jnp.zeros(op_in.shape[2:], jnp.float32)
        totals = lax.fori_loop(0, devices, add, (zero,) * relations, unroll=4)
        for relation in range(relations):
            gathered[my_reducer, relation] = (totals[relation] * scale).astype(jnp.bfloat16)

        piece = gathered.at[my_reducer]

        @pl.loop(1, n_rows // PLANE)
        def _(step):
            row = lax.rem(my_row + step * PLANE, n_rows)
            remote(piece, piece, fan_sem.at[PLANE + step], gather_sem.at[my_reducer], row, my_rep).start()

        for step in range(1, PLANE):
            row = lax.div(my_row, PLANE) * PLANE + lax.rem(my_row + step, PLANE)
            remote(piece, piece, fan_sem.at[step], gather_sem.at[my_reducer], row, my_rep).start()

        remote(piece, piece, fan_sem.at[0], gather_sem.at[my_reducer], my_row, other_rep).start()

    settle(grad_in, receive_sem.at[4])
    all_rows = column(requests[...], 0).astype(jnp.int32)
    grads = unpack(grad_in[...]).astype(jnp.bfloat16)
    half = entity_ref.shape[0]

    @pl.loop(0, half // step_rows)
    def _(step):
        first = pl.multiple_of(step * step_rows, step_rows)
        lane = lax.broadcasted_iota(jnp.int32, (all_rows.shape[0], step_rows), 1) + first + my_rep * half
        place = (all_rows == lane).astype(jnp.float32).astype(jnp.bfloat16)
        entity_ref[pl.ds(first, step_rows), :] = dot(place, grads, 0, 0).astype(jnp.bfloat16)

    entity_copy = pltpu.make_async_copy(entity_ref, entity_hbm, local_sem.at[6])
    entity_copy.start()

    def mine(reducer):
        device = reducer * stride
        same_rep = lax.rem(device, n_rep) == my_rep
        same_column = lax.rem(lax.div(device, n_rep), PLANE) == lax.rem(my_row, PLANE)
        first = jnp.logical_and(jnp.logical_and(same_rep, same_column), device != me)
        second = jnp.logical_and(same_rep, jnp.logical_not(same_column))
        return first, second

    @pl.loop(0, reducers)
    def _(step):
        reducer = lax.rem(my_reducer + 1 + step, reducers)
        piece = gathered.at[reducer]

        @pl.when(mine(reducer)[0])
        def _():
            settle(piece, gather_sem.at[reducer])
            for hop in range(1, PLANE):
                row = lax.div(my_row, PLANE) * PLANE + lax.rem(my_row + hop, PLANE)
                remote(piece, piece, pass_sem.at[reducer, hop], gather_sem.at[reducer], row, my_rep).start()
            remote(piece, piece, pass_sem.at[reducer, 0], gather_sem.at[reducer], my_row, other_rep).start()

    @pl.loop(0, reducers)
    def _(step):
        reducer = lax.rem(my_reducer + 1 + step, reducers)
        piece = gathered.at[reducer]

        @pl.when(mine(reducer)[1])
        def _():
            settle(piece, gather_sem.at[reducer])
            remote(piece, piece, pass_sem.at[reducer, 0], gather_sem.at[reducer], my_row, other_rep).start()

    @pl.loop(0, reducers // 2)
    def _(pair):
        halves = []
        for reducer in (2 * pair, 2 * pair + 1):

            @pl.when(lax.rem(reducer * stride, n_rep) != my_rep)
            def _():
                settle(gathered.at[reducer], gather_sem.at[reducer])

            rows = gathered[reducer].astype(jnp.float32)
            halves.append(jnp.concatenate([rows[:, :TILE, :], rows[:, TILE:, :]], axis=2))
        first = pl.multiple_of(pair * 2 * TILE, 2 * TILE)
        relation_out[:, pl.ds(first, 2 * TILE), :] = jnp.concatenate(halves, axis=1).astype(jnp.bfloat16)

    settle(head_ref.at[pl.ds(0, n_rows - 1)], send_sem.at[0])
    settle(head_ref, send_sem.at[1])
    settle(served.at[pl.ds(0, n_rows - 1)], send_sem.at[2])
    settle(op_out.at[pl.ds(0, reducers - 1)], send_sem.at[3])

    @pl.when(jnp.logical_not(reducing))
    def _():
        settle(op_out.at[0], send_sem.at[3])

    settle(grad_in.at[pl.ds(0, devices - 1)], send_sem.at[4])

    @pl.when(reducing)
    def _():
        for step in range(PLANE):
            settle(gathered.at[my_reducer], fan_sem.at[step])

        @pl.loop(1, n_rows // PLANE)
        def _(step):
            settle(gathered.at[my_reducer], fan_sem.at[PLANE + step])

    @pl.loop(0, reducers)
    def _(reducer):
        first, second = mine(reducer)

        @pl.when(jnp.logical_or(first, second))
        def _():
            settle(gathered.at[reducer], pass_sem.at[reducer, 0])

        @pl.when(first)
        def _():
            for hop in range(1, PLANE):
                settle(gathered.at[reducer], pass_sem.at[reducer, hop])

    entity_copy.wait()


def shards(
    entity_table, relation_ops, need_rows, send_offsets, source_ids, target_ids, negative_ids, relation_ids
):
    n_rows, n_rep = lax.axis_size("rows"), lax.axis_size("rep")
    devices = n_rows * n_rep
    need = need_rows[0, 0]
    capacity = need.shape[1]
    blocks, edges = source_ids.shape[2:]
    relations, width, _ = relation_ops.shape
    reducers = width // TILE
    scale = (relations / (edges * blocks * devices)) ** 0.5
    packed = (2 * TILE, LANES)
    slots = n_rows * capacity
    hbm = pl.BlockSpec(memory_space=pltpu.HBM)
    smem = pl.BlockSpec(memory_space=pltpu.SMEM)
    entity_shape = (entity_table.shape[0] // n_rep, width)
    entity_grad, relation_grad = pl.pallas_call(
        functools.partial(kernel, n_rows, n_rep, scale),
        out_shape=(
            jax.ShapeDtypeStruct(entity_shape, jnp.bfloat16),
            jax.ShapeDtypeStruct(relation_ops.shape, jnp.bfloat16),
        ),
        in_specs=[smem, smem] + [hbm] * 6,
        out_specs=(hbm, pl.BlockSpec(memory_space=pltpu.VMEM)),
        scratch_shapes=[
            pltpu.VMEM((capacity, n_rows), jnp.int32),
            pltpu.VMEM((blocks, edges), jnp.int32),
            pltpu.VMEM((blocks, edges), jnp.int32),
            pltpu.VMEM((blocks, negative_ids.shape[-1]), jnp.int32),
            pltpu.VMEM((n_rows, 1, LANES), jnp.int32),
            pltpu.VMEM((slots, LANES), jnp.int32),
            pltpu.VMEM(entity_shape, jnp.bfloat16),
            pltpu.VMEM(entity_table.shape, jnp.bfloat16),
            pltpu.VMEM(relation_ops.shape, jnp.bfloat16),
            pltpu.VMEM((devices, 1, LANES), jnp.int32),
            pltpu.VMEM((n_rows, *packed), jnp.bfloat16),
            pltpu.VMEM((n_rows, *packed), jnp.bfloat16),
            pltpu.VMEM((n_rows, *packed), jnp.bfloat16),
            pltpu.VMEM((devices, *packed), jnp.bfloat16),
            pltpu.VMEM((reducers, blocks, *packed), jnp.bfloat16),
            pltpu.VMEM((devices, blocks, *packed), jnp.bfloat16),
            pltpu.VMEM((blocks, devices, 1, LANES), jnp.float32),
            pltpu.VMEM((reducers, relations, *packed), jnp.bfloat16),
            pltpu.VMEM((blocks, slots, slots), jnp.float32),
            pltpu.VMEM((blocks, TILE, slots), jnp.float32),
            pltpu.VMEM((slots, width), jnp.float32),
            pltpu.SemaphoreType.DMA((7,)),
            pltpu.SemaphoreType.DMA((5,)),
            pltpu.SemaphoreType.DMA((5,)),
            pltpu.SemaphoreType.DMA((reducers,)),
            pltpu.SemaphoreType.DMA((PLANE + n_rows // PLANE,)),
            pltpu.SemaphoreType.DMA((reducers, PLANE)),
        ],
        compiler_params=pltpu.CompilerParams(
            collective_id=0, has_side_effects=True, vmem_limit_bytes=64 * 1024 * 1024 - 16384
        ),
    )(
        relation_ids[0, 0], send_offsets[0, 0], need.T, source_ids[0, 0], target_ids[0, 0], negative_ids[0, 0],
        entity_table, relation_ops,
    )
    return entity_grad, relation_grad.astype(jnp.float32)


def solution(mesh):
    return jax.shard_map(
        shards,
        mesh=mesh,
        in_specs=(
            P("rows", None),
            P(),
            P("rows", "rep", None, None),
            P("rows", "rep", None),
            P("rows", "rep", None, None),
            P("rows", "rep", None, None),
            P("rows", "rep", None, None),
            P("rows", "rep", None),
        ),
        out_specs=(P(("rows", "rep"), None), P()),
        check_vma=False,
    )
```

```python
import functools

import jax
import jax.numpy as jnp
from jax import lax
from jax.experimental import pallas as pl
from jax.experimental.pallas import tpu as pltpu
from jax.sharding import PartitionSpec as P

LANES = 128
TILE = 8
REL_LANE = 16
PLANE = 4


def pack(rows):
    cubes = rows.reshape(rows.shape[0] // TILE, TILE, rows.shape[1])
    return jnp.concatenate([cubes[:, :, :LANES], cubes[:, :, LANES:]], axis=1).astype(jnp.bfloat16)


def unpack(packed):
    wide = packed.astype(jnp.float32)
    joined = jnp.concatenate([wide[:, :TILE, :], wide[:, TILE:, :]], axis=2)
    return joined.reshape(joined.shape[0] * TILE, joined.shape[2])


def column(messages, first_lane):
    count = messages.shape[0]
    wide = jnp.broadcast_to(messages.astype(jnp.float32), (count, TILE, LANES)).reshape(count * TILE, LANES)
    lane = lax.broadcasted_iota(jnp.int32, wide.shape, 1)
    row = lax.rem(lax.broadcasted_iota(jnp.int32, wide.shape, 0), TILE)
    return jnp.sum(jnp.where(lane == row + first_lane, wide, 0.0), axis=1, keepdims=True)


def dot(left, right, left_dim, right_dim):
    return lax.dot_general(
        left, right, (((left_dim,), (right_dim,)), ((), ())), preferred_element_type=jnp.float32
    )


def split(value):
    upper = value.astype(jnp.bfloat16)
    return upper, (value - upper.astype(jnp.float32)).astype(jnp.bfloat16)


def kernel(
    n_rows, n_rep, scale,
    relation_ref, offset_ref, need_hbm, source_hbm, target_hbm, negative_hbm, table_hbm, ops_hbm,
    entity_hbm, relation_out,
    need_ref, source_ref, target_ref, negative_ref, head_ref, compact_ref, entity_ref,
    table, operators, requests, served, slots_in, grad_out, grad_in, op_out, op_in, relation_of, gathered,
    pair_count, negative_count, row_acc,
    local_sem, send_sem, receive_sem, gather_sem, fan_sem, pass_sem,
):
    devices = n_rows * n_rep
    my_row, my_rep = lax.axis_index("rows"), lax.axis_index("rep")
    me = my_row * n_rep + my_rep
    my_slot = my_rep * n_rows + my_row
    other_rep = n_rep - 1 - my_rep
    blocks = source_ref.shape[0]
    relations, width, _ = operators.shape
    reducers = width // TILE
    stride = devices // reducers
    weight_neg = negative_ref.shape[1] ** (-0.5)

    table_copy = pltpu.make_async_copy(table_hbm, table, local_sem.at[0])
    table_copy.start()
    ops_copy = pltpu.make_async_copy(ops_hbm, operators, local_sem.at[1])
    ops_copy.start()
    need_copy = pltpu.make_async_copy(need_hbm, need_ref, local_sem.at[2])
    need_copy.start()
    id_copies = [
        pltpu.make_async_copy(hbm, ref, local_sem.at[3 + index])
        for index, (hbm, ref) in enumerate(
            ((source_hbm, source_ref), (target_hbm, target_ref), (negative_hbm, negative_ref))
        )
    ]
    for id_copy in id_copies:
        id_copy.start()

    def remote(source, destination, send, receive, row, rep):
        return pltpu.make_async_remote_copy(
            src_ref=source, dst_ref=destination, send_sem=send, recv_sem=receive,
            device_id=(row, rep), device_id_type=pl.DeviceIdType.MESH,
        )

    def settle(buffer, semaphore):
        pltpu.make_async_copy(buffer, buffer, semaphore).wait()

    barrier = pltpu.get_barrier_semaphore()

    @pl.loop(1, devices)
    def _(step):
        other = lax.rem(me + step, devices)
        pl.semaphore_signal(
            barrier, inc=1, device_id=(lax.div(other, n_rep), lax.rem(other, n_rep)),
            device_id_type=pl.DeviceIdType.MESH,
        )

    lane = lax.broadcasted_iota(jnp.int32, (TILE, LANES), 1)
    sublane = lax.broadcasted_iota(jnp.int32, (TILE, LANES), 0)
    kinds = jnp.zeros((1, LANES), jnp.int32)
    for block in range(blocks):
        kinds = jnp.where(lane[:1] == REL_LANE + block, relation_ref[block], kinds)
    need_copy.wait()
    need = need_ref[...].astype(jnp.float32)
    for row in range(n_rows):
        wide = jnp.where(lane == sublane, jnp.broadcast_to(need[:, row : row + 1], lane.shape), 0.0)
        head_ref[row] = jnp.sum(wide, axis=0, keepdims=True).astype(jnp.int32) + kinds
        first_id = offset_ref[row]
        slot_id = first_id + sublane
        compact_ref[row * TILE : (row + 1) * TILE, :] = jnp.where(slot_id < offset_ref[row + 1], slot_id, -1)

    pl.semaphore_wait(barrier, devices - 1)

    own_request = pltpu.make_async_copy(head_ref.at[my_row], requests.at[my_slot], receive_sem.at[0])
    own_request.start()

    @pl.loop(1, n_rows)
    def _(step):
        row = lax.rem(my_row + step, n_rows)
        remote(head_ref.at[row], requests.at[my_slot], send_sem.at[0], receive_sem.at[0], row, my_rep).start()

    @pl.loop(0, n_rows)
    def _(step):
        row = lax.rem(my_row + step, n_rows)
        remote(head_ref.at[row], requests.at[my_slot], send_sem.at[1], receive_sem.at[1], row, other_rep).start()

    for id_copy in id_copies:
        id_copy.wait()
    compact = compact_ref[:, :1]
    for block in range(blocks):
        hit = [
            (compact == ids[block : block + 1, :]).astype(jnp.float32).astype(jnp.bfloat16)
            for ids in (source_ref, target_ref, negative_ref)
        ]
        pair_count[block] = dot(hit[0], hit[1], 1, 1)
        ones = jnp.ones((TILE, hit[2].shape[1]), jnp.bfloat16)
        negative_count[block] = dot(ones, hit[2], 1, 1)

    settle(requests.at[pl.ds(my_rep * n_rows, n_rows)], receive_sem.at[0])
    wanted = column(requests[pl.ds(my_rep * n_rows, n_rows)], 0).astype(jnp.int32)
    table_copy.wait()
    step_rows = 512
    row_acc[...] = jnp.zeros_like(row_acc)

    @pl.loop(0, table.shape[0] // step_rows, unroll=4)
    def _(step):
        first = pl.multiple_of(step * step_rows, step_rows)
        lane = lax.broadcasted_iota(jnp.int32, (wanted.shape[0], step_rows), 1) + first
        pick = (wanted == lane).astype(jnp.float32).astype(jnp.bfloat16)
        row_acc[...] += dot(pick, table[pl.ds(first, step_rows), :], 1, 0)

    served[...] = pack(row_acc[...])
    own_rows = pltpu.make_async_copy(served.at[my_row], slots_in.at[my_row], receive_sem.at[2])
    own_rows.start()

    @pl.loop(1, n_rows)
    def _(step):
        row = lax.rem(my_row + step, n_rows)
        remote(served.at[row], slots_in.at[my_row], send_sem.at[2], receive_sem.at[2], row, my_rep).start()

    settle(requests.at[pl.ds(other_rep * n_rows, n_rows)], receive_sem.at[1])
    heads = requests[...].astype(jnp.float32)
    head_lane = lax.broadcasted_iota(jnp.int32, heads.shape, 2)
    for block in range(blocks):
        kind = jnp.sum(jnp.where(head_lane == REL_LANE + block, heads, 0.0), axis=2, keepdims=True)
        relation_of[block] = jnp.broadcast_to(kind, heads.shape)
    ops_copy.wait()
    settle(slots_in, receive_sem.at[2])

    slots = unpack(slots_in[...]).astype(jnp.bfloat16)
    slot_grad = jnp.zeros(slots.shape, jnp.float32)
    for block in range(blocks):
        operator = operators[relation_ref[block]]
        query = dot(slots, operator, 1, 0).astype(jnp.bfloat16)
        scores = dot(query, slots, 1, 1)
        pairs = pair_count[block]
        source_count = jnp.sum(pairs, axis=1, keepdims=True)
        coefficient = source_count * negative_count[block][:1, :] * (jax.nn.sigmoid(scores) * weight_neg)
        coefficient = coefficient - pairs * jax.nn.sigmoid(-scores)
        upper, lower = split(coefficient)
        query_grad = (dot(upper, slots, 1, 0) + dot(lower, slots, 1, 0)).astype(jnp.bfloat16)
        op_out[:, block] = pack(dot(slots, query_grad, 0, 0))
        slot_grad = slot_grad + dot(query_grad, operator, 1, 1)
        slot_grad = slot_grad + dot(upper, query, 0, 0) + dot(lower, query, 0, 0)
    grad_out[...] = pack(slot_grad)

    my_reducer = lax.div(me, stride)
    reducing = lax.rem(me, stride) == 0

    @pl.loop(0, reducers)
    def _(step):
        reducer = lax.rem(my_reducer + 1 + step, reducers)
        device = reducer * stride

        @pl.when(device != me)
        def _():
            remote(
                op_out.at[reducer], op_in.at[my_slot], send_sem.at[3], receive_sem.at[3],
                lax.div(device, n_rep), lax.rem(device, n_rep),
            ).start()

        @pl.when(device == me)
        def _():
            pltpu.make_async_copy(op_out.at[reducer], op_in.at[my_slot], receive_sem.at[3]).start()

    pltpu.make_async_copy(grad_out.at[my_row], grad_in.at[my_slot], receive_sem.at[4]).start()

    @pl.loop(1, devices)
    def _(step):
        device = lax.rem(me + step, devices)
        row = lax.div(device, n_rep)
        remote(
            grad_out.at[row], grad_in.at[my_slot], send_sem.at[4], receive_sem.at[4], row, lax.rem(device, n_rep)
        ).start()

    @pl.when(reducing)
    def _():
        settle(op_in, receive_sem.at[3])

        def add(source, totals):
            totals = list(totals)
            for block in range(blocks):
                term = op_in[source, block].astype(jnp.float32)
                kind = relation_of[block, source]
                for relation in range(relations):
                    totals[relation] = totals[relation] + jnp.where(kind == float(relation), term, 0.0)
            return tuple(totals)

        zero = jnp.zeros(op_in.shape[2:], jnp.float32)
        totals = lax.fori_loop(0, devices, add, (zero,) * relations, unroll=4)
        for relation in range(relations):
            gathered[my_reducer, relation] = (totals[relation] * scale).astype(jnp.bfloat16)

        piece = gathered.at[my_reducer]

        @pl.loop(1, n_rows // PLANE)
        def _(step):
            row = lax.rem(my_row + step * PLANE, n_rows)
            remote(piece, piece, fan_sem.at[PLANE + step], gather_sem.at[my_reducer], row, my_rep).start()

        for step in range(1, PLANE):
            row = lax.div(my_row, PLANE) * PLANE + lax.rem(my_row + step, PLANE)
            remote(piece, piece, fan_sem.at[step], gather_sem.at[my_reducer], row, my_rep).start()

        remote(piece, piece, fan_sem.at[0], gather_sem.at[my_reducer], my_row, other_rep).start()

    def mine(reducer):
        device = reducer * stride
        same_rep = lax.rem(device, n_rep) == my_rep
        same_column = lax.rem(lax.div(device, n_rep), PLANE) == lax.rem(my_row, PLANE)
        first = jnp.logical_and(jnp.logical_and(same_rep, same_column), device != me)
        second = jnp.logical_and(same_rep, jnp.logical_not(same_column))
        return first, second

    @pl.loop(0, reducers)
    def _(step):
        reducer = lax.rem(my_reducer + 1 + step, reducers)
        piece = gathered.at[reducer]

        @pl.when(mine(reducer)[0])
        def _():
            settle(piece, gather_sem.at[reducer])
            for hop in range(1, PLANE):
                row = lax.div(my_row, PLANE) * PLANE + lax.rem(my_row + hop, PLANE)
                remote(piece, piece, pass_sem.at[reducer, hop], gather_sem.at[reducer], row, my_rep).start()
            remote(piece, piece, pass_sem.at[reducer, 0], gather_sem.at[reducer], my_row, other_rep).start()

    settle(grad_in, receive_sem.at[4])
    all_rows = column(requests[...], 0).astype(jnp.int32)
    grads = unpack(grad_in[...]).astype(jnp.bfloat16)
    half = entity_ref.shape[0]

    @pl.loop(0, half // step_rows, unroll=2)
    def _(step):
        first = pl.multiple_of(step * step_rows, step_rows)
        lane = lax.broadcasted_iota(jnp.int32, (all_rows.shape[0], step_rows), 1) + first + my_rep * half
        place = (all_rows == lane).astype(jnp.float32).astype(jnp.bfloat16)
        entity_ref[pl.ds(first, step_rows), :] = dot(place, grads, 0, 0).astype(jnp.bfloat16)

    entity_copy = pltpu.make_async_copy(entity_ref, entity_hbm, local_sem.at[6])
    entity_copy.start()

    @pl.loop(0, reducers)
    def _(step):
        reducer = lax.rem(my_reducer + 1 + step, reducers)
        piece = gathered.at[reducer]

        @pl.when(mine(reducer)[1])
        def _():
            settle(piece, gather_sem.at[reducer])
            remote(piece, piece, pass_sem.at[reducer, 0], gather_sem.at[reducer], my_row, other_rep).start()

    @pl.loop(0, reducers // 2)
    def _(pair):
        halves = []
        for reducer in (2 * pair, 2 * pair + 1):

            @pl.when(lax.rem(reducer * stride, n_rep) != my_rep)
            def _():
                settle(gathered.at[reducer], gather_sem.at[reducer])

            rows = gathered[reducer].astype(jnp.float32)
            halves.append(jnp.concatenate([rows[:, :TILE, :], rows[:, TILE:, :]], axis=2))
        first = pl.multiple_of(pair * 2 * TILE, 2 * TILE)
        relation_out[:, pl.ds(first, 2 * TILE), :] = jnp.concatenate(halves, axis=1).astype(jnp.bfloat16)

    settle(head_ref.at[pl.ds(0, n_rows - 1)], send_sem.at[0])
    settle(head_ref, send_sem.at[1])
    settle(served.at[pl.ds(0, n_rows - 1)], send_sem.at[2])
    settle(op_out.at[pl.ds(0, reducers - 1)], send_sem.at[3])

    @pl.when(jnp.logical_not(reducing))
    def _():
        settle(op_out.at[0], send_sem.at[3])

    settle(grad_in.at[pl.ds(0, devices - 1)], send_sem.at[4])

    @pl.when(reducing)
    def _():
        for step in range(PLANE):
            settle(gathered.at[my_reducer], fan_sem.at[step])

        @pl.loop(1, n_rows // PLANE)
        def _(step):
            settle(gathered.at[my_reducer], fan_sem.at[PLANE + step])

    @pl.loop(0, reducers)
    def _(reducer):
        first, second = mine(reducer)

        @pl.when(jnp.logical_or(first, second))
        def _():
            settle(gathered.at[reducer], pass_sem.at[reducer, 0])

        @pl.when(first)
        def _():
            for hop in range(1, PLANE):
                settle(gathered.at[reducer], pass_sem.at[reducer, hop])

    entity_copy.wait()


def shards(
    entity_table, relation_ops, need_rows, send_offsets, source_ids, target_ids, negative_ids, relation_ids
):
    n_rows, n_rep = lax.axis_size("rows"), lax.axis_size("rep")
    devices = n_rows * n_rep
    need = need_rows[0, 0]
    capacity = need.shape[1]
    blocks, edges = source_ids.shape[2:]
    relations, width, _ = relation_ops.shape
    reducers = width // TILE
    scale = (relations / (edges * blocks * devices)) ** 0.5
    packed = (2 * TILE, LANES)
    slots = n_rows * capacity
    hbm = pl.BlockSpec(memory_space=pltpu.HBM)
    smem = pl.BlockSpec(memory_space=pltpu.SMEM)
    entity_shape = (entity_table.shape[0] // n_rep, width)
    entity_grad, relation_grad = pl.pallas_call(
        functools.partial(kernel, n_rows, n_rep, scale),
        out_shape=(
            jax.ShapeDtypeStruct(entity_shape, jnp.bfloat16),
            jax.ShapeDtypeStruct(relation_ops.shape, jnp.bfloat16),
        ),
        in_specs=[smem, smem] + [hbm] * 6,
        out_specs=(hbm, pl.BlockSpec(memory_space=pltpu.VMEM)),
        scratch_shapes=[
            pltpu.VMEM((capacity, n_rows), jnp.int32),
            pltpu.VMEM((blocks, edges), jnp.int32),
            pltpu.VMEM((blocks, edges), jnp.int32),
            pltpu.VMEM((blocks, negative_ids.shape[-1]), jnp.int32),
            pltpu.VMEM((n_rows, 1, LANES), jnp.int32),
            pltpu.VMEM((slots, LANES), jnp.int32),
            pltpu.VMEM(entity_shape, jnp.bfloat16),
            pltpu.VMEM(entity_table.shape, jnp.bfloat16),
            pltpu.VMEM(relation_ops.shape, jnp.bfloat16),
            pltpu.VMEM((devices, 1, LANES), jnp.int32),
            pltpu.VMEM((n_rows, *packed), jnp.bfloat16),
            pltpu.VMEM((n_rows, *packed), jnp.bfloat16),
            pltpu.VMEM((n_rows, *packed), jnp.bfloat16),
            pltpu.VMEM((devices, *packed), jnp.bfloat16),
            pltpu.VMEM((reducers, blocks, *packed), jnp.bfloat16),
            pltpu.VMEM((devices, blocks, *packed), jnp.bfloat16),
            pltpu.VMEM((blocks, devices, 1, LANES), jnp.float32),
            pltpu.VMEM((reducers, relations, *packed), jnp.bfloat16),
            pltpu.VMEM((blocks, slots, slots), jnp.float32),
            pltpu.VMEM((blocks, TILE, slots), jnp.float32),
            pltpu.VMEM((slots, width), jnp.float32),
            pltpu.SemaphoreType.DMA((7,)),
            pltpu.SemaphoreType.DMA((5,)),
            pltpu.SemaphoreType.DMA((5,)),
            pltpu.SemaphoreType.DMA((reducers,)),
            pltpu.SemaphoreType.DMA((PLANE + n_rows // PLANE,)),
            pltpu.SemaphoreType.DMA((reducers, PLANE)),
        ],
        compiler_params=pltpu.CompilerParams(
            collective_id=0, has_side_effects=True, vmem_limit_bytes=64 * 1024 * 1024 - 16384
        ),
    )(
        relation_ids[0, 0], send_offsets[0, 0], need.T, source_ids[0, 0], target_ids[0, 0], negative_ids[0, 0],
        entity_table, relation_ops,
    )
    return entity_grad, relation_grad.astype(jnp.float32)


def solution(mesh):
    return jax.shard_map(
        shards,
        mesh=mesh,
        in_specs=(
            P("rows", None),
            P(),
            P("rows", "rep", None, None),
            P("rows", "rep", None),
            P("rows", "rep", None, None),
            P("rows", "rep", None, None),
            P("rows", "rep", None, None),
            P("rows", "rep", None),
        ),
        out_specs=(P(("rows", "rep"), None), P()),
        check_vma=False,
    )
```

```python
import functools

import jax
import jax.numpy as jnp
from jax import lax
from jax.experimental import pallas as pl
from jax.experimental.pallas import tpu as pltpu
from jax.sharding import PartitionSpec as P

LANES = 128
TILE = 8
REL_LANE = 16
PLANE = 4


def pack(rows):
    cubes = rows.reshape(rows.shape[0] // TILE, TILE, rows.shape[1])
    return jnp.concatenate([cubes[:, :, :LANES], cubes[:, :, LANES:]], axis=1).astype(jnp.bfloat16)


def unpack(packed):
    wide = packed.astype(jnp.float32)
    joined = jnp.concatenate([wide[:, :TILE, :], wide[:, TILE:, :]], axis=2)
    return joined.reshape(joined.shape[0] * TILE, joined.shape[2])


def column(messages, first_lane):
    count = messages.shape[0]
    wide = jnp.broadcast_to(messages.astype(jnp.float32), (count, TILE, LANES)).reshape(count * TILE, LANES)
    lane = lax.broadcasted_iota(jnp.int32, wide.shape, 1)
    row = lax.rem(lax.broadcasted_iota(jnp.int32, wide.shape, 0), TILE)
    return jnp.sum(jnp.where(lane == row + first_lane, wide, 0.0), axis=1, keepdims=True)


def dot(left, right, left_dim, right_dim):
    return lax.dot_general(
        left, right, (((left_dim,), (right_dim,)), ((), ())), preferred_element_type=jnp.float32
    )


def split(value):
    upper = value.astype(jnp.bfloat16)
    return upper, (value - upper.astype(jnp.float32)).astype(jnp.bfloat16)


def kernel(
    n_rows, n_rep, scale,
    relation_ref, offset_ref, need_hbm, source_hbm, target_hbm, negative_hbm, table_hbm, ops_hbm,
    entity_hbm, relation_out,
    need_ref, source_ref, target_ref, negative_ref, head_ref, compact_ref, entity_ref,
    table, operators, requests, served, slots_in, grad_out, grad_in, op_out, op_in, relation_of, gathered,
    pair_count, negative_count, row_acc,
    local_sem, send_sem, receive_sem, gather_sem, fan_sem, pass_sem,
):
    devices = n_rows * n_rep
    my_row, my_rep = lax.axis_index("rows"), lax.axis_index("rep")
    me = my_row * n_rep + my_rep
    my_slot = my_rep * n_rows + my_row
    other_rep = n_rep - 1 - my_rep
    blocks = source_ref.shape[0]
    relations, width, _ = operators.shape
    reducers = width // TILE
    stride = devices // reducers
    weight_neg = negative_ref.shape[1] ** (-0.5)

    table_copy = pltpu.make_async_copy(table_hbm, table, local_sem.at[0])
    table_copy.start()
    ops_copy = pltpu.make_async_copy(ops_hbm, operators, local_sem.at[1])
    ops_copy.start()
    need_copy = pltpu.make_async_copy(need_hbm, need_ref, local_sem.at[2])
    need_copy.start()
    id_copies = [
        pltpu.make_async_copy(hbm, ref, local_sem.at[3 + index])
        for index, (hbm, ref) in enumerate(
            ((source_hbm, source_ref), (target_hbm, target_ref), (negative_hbm, negative_ref))
        )
    ]
    for id_copy in id_copies:
        id_copy.start()

    def remote(source, destination, send, receive, row, rep):
        return pltpu.make_async_remote_copy(
            src_ref=source, dst_ref=destination, send_sem=send, recv_sem=receive,
            device_id=(row, rep), device_id_type=pl.DeviceIdType.MESH,
        )

    def settle(buffer, semaphore):
        pltpu.make_async_copy(buffer, buffer, semaphore).wait()

    barrier = pltpu.get_barrier_semaphore()

    @pl.loop(1, devices)
    def _(step):
        other = lax.rem(me + step, devices)
        pl.semaphore_signal(
            barrier, inc=1, device_id=(lax.div(other, n_rep), lax.rem(other, n_rep)),
            device_id_type=pl.DeviceIdType.MESH,
        )

    lane = lax.broadcasted_iota(jnp.int32, (TILE, LANES), 1)
    sublane = lax.broadcasted_iota(jnp.int32, (TILE, LANES), 0)
    kinds = jnp.zeros((1, LANES), jnp.int32)
    for block in range(blocks):
        kinds = jnp.where(lane[:1] == REL_LANE + block, relation_ref[block], kinds)
    need_copy.wait()
    need = need_ref[...].astype(jnp.float32)
    for row in range(n_rows):
        wide = jnp.where(lane == sublane, jnp.broadcast_to(need[:, row : row + 1], lane.shape), 0.0)
        head_ref[row] = jnp.sum(wide, axis=0, keepdims=True).astype(jnp.int32) + kinds
        first_id = offset_ref[row]
        slot_id = first_id + sublane
        compact_ref[row * TILE : (row + 1) * TILE, :] = jnp.where(slot_id < offset_ref[row + 1], slot_id, -1)

    pl.semaphore_wait(barrier, devices - 1)

    own_request = pltpu.make_async_copy(head_ref.at[my_row], requests.at[my_slot], receive_sem.at[0])
    own_request.start()

    @pl.loop(1, n_rows)
    def _(step):
        row = lax.rem(my_row + step, n_rows)
        remote(head_ref.at[row], requests.at[my_slot], send_sem.at[0], receive_sem.at[0], row, my_rep).start()

    @pl.loop(0, n_rows)
    def _(step):
        row = lax.rem(my_row + step, n_rows)
        remote(head_ref.at[row], requests.at[my_slot], send_sem.at[1], receive_sem.at[1], row, other_rep).start()

    for id_copy in id_copies:
        id_copy.wait()
    compact = compact_ref[:, :1]
    for block in range(blocks):
        hit = [
            (compact == ids[block : block + 1, :]).astype(jnp.float32).astype(jnp.bfloat16)
            for ids in (source_ref, target_ref, negative_ref)
        ]
        pair_count[block] = dot(hit[0], hit[1], 1, 1)
        ones = jnp.ones((TILE, hit[2].shape[1]), jnp.bfloat16)
        negative_count[block] = dot(ones, hit[2], 1, 1)

    settle(requests.at[pl.ds(my_rep * n_rows, n_rows)], receive_sem.at[0])
    wanted = column(requests[pl.ds(my_rep * n_rows, n_rows)], 0).astype(jnp.int32)
    table_copy.wait()
    step_rows = 512
    row_acc[...] = jnp.zeros_like(row_acc)

    @pl.loop(0, table.shape[0] // step_rows, unroll=4)
    def _(step):
        first = pl.multiple_of(step * step_rows, step_rows)
        lane = lax.broadcasted_iota(jnp.int32, (wanted.shape[0], step_rows), 1) + first
        pick = (wanted == lane).astype(jnp.float32).astype(jnp.bfloat16)
        row_acc[...] += dot(pick, table[pl.ds(first, step_rows), :], 1, 0)

    served[...] = pack(row_acc[...])
    own_rows = pltpu.make_async_copy(served.at[my_row], slots_in.at[my_row], receive_sem.at[2])
    own_rows.start()

    @pl.loop(1, n_rows)
    def _(step):
        row = lax.rem(my_row + step, n_rows)
        remote(served.at[row], slots_in.at[my_row], send_sem.at[2], receive_sem.at[2], row, my_rep).start()

    settle(requests.at[pl.ds(other_rep * n_rows, n_rows)], receive_sem.at[1])
    heads = requests[...].astype(jnp.float32)
    head_lane = lax.broadcasted_iota(jnp.int32, heads.shape, 2)
    for block in range(blocks):
        kind = jnp.sum(jnp.where(head_lane == REL_LANE + block, heads, 0.0), axis=2, keepdims=True)
        relation_of[block] = jnp.broadcast_to(kind, heads.shape)
    ops_copy.wait()
    settle(slots_in, receive_sem.at[2])

    slots = unpack(slots_in[...]).astype(jnp.bfloat16)
    slot_grad = jnp.zeros(slots.shape, jnp.float32)
    for block in range(blocks):
        operator = operators[relation_ref[block]]
        query = dot(slots, operator, 1, 0).astype(jnp.bfloat16)
        scores = dot(query, slots, 1, 1)
        pairs = pair_count[block]
        source_count = jnp.sum(pairs, axis=1, keepdims=True)
        coefficient = source_count * negative_count[block][:1, :] * (jax.nn.sigmoid(scores) * weight_neg)
        coefficient = coefficient - pairs * jax.nn.sigmoid(-scores)
        upper, lower = split(coefficient)
        query_grad = (dot(upper, slots, 1, 0) + dot(lower, slots, 1, 0)).astype(jnp.bfloat16)
        op_out[:, block] = pack(dot(slots, query_grad, 0, 0))
        slot_grad = slot_grad + dot(query_grad, operator, 1, 1)
        slot_grad = slot_grad + dot(upper, query, 0, 0) + dot(lower, query, 0, 0)
    grad_out[...] = pack(slot_grad)

    my_reducer = lax.div(me, stride)
    reducing = lax.rem(me, stride) == 0

    @pl.loop(0, reducers)
    def _(step):
        reducer = lax.rem(my_reducer + 1 + step, reducers)
        device = reducer * stride

        @pl.when(device != me)
        def _():
            remote(
                op_out.at[reducer], op_in.at[my_slot], send_sem.at[3], receive_sem.at[3],
                lax.div(device, n_rep), lax.rem(device, n_rep),
            ).start()

        @pl.when(device == me)
        def _():
            pltpu.make_async_copy(op_out.at[reducer], op_in.at[my_slot], receive_sem.at[3]).start()

    pltpu.make_async_copy(grad_out.at[my_row], grad_in.at[my_slot], receive_sem.at[4]).start()

    @pl.loop(1, devices)
    def _(step):
        device = lax.rem(me + step, devices)
        row = lax.div(device, n_rep)
        remote(
            grad_out.at[row], grad_in.at[my_slot], send_sem.at[4], receive_sem.at[4], row, lax.rem(device, n_rep)
        ).start()

    @pl.when(reducing)
    def _():
        settle(op_in, receive_sem.at[3])

        def add(source, totals):
            totals = list(totals)
            for block in range(blocks):
                term = op_in[source, block].astype(jnp.float32)
                kind = relation_of[block, source]
                for relation in range(relations):
                    totals[relation] = totals[relation] + jnp.where(kind == float(relation), term, 0.0)
            return tuple(totals)

        zero = jnp.zeros(op_in.shape[2:], jnp.float32)
        totals = lax.fori_loop(0, devices, add, (zero,) * relations, unroll=4)
        for relation in range(relations):
            gathered[my_reducer, relation] = (totals[relation] * scale).astype(jnp.bfloat16)

        piece = gathered.at[my_reducer]

        @pl.loop(1, n_rows // PLANE)
        def _(step):
            row = lax.rem(my_row + step * PLANE, n_rows)
            remote(piece, piece, fan_sem.at[PLANE + step], gather_sem.at[my_reducer], row, my_rep).start()

        for step in range(1, PLANE):
            row = lax.div(my_row, PLANE) * PLANE + lax.rem(my_row + step, PLANE)
            remote(piece, piece, fan_sem.at[step], gather_sem.at[my_reducer], row, my_rep).start()

        remote(piece, piece, fan_sem.at[0], gather_sem.at[my_reducer], my_row, other_rep).start()

    def mine(reducer):
        device = reducer * stride
        same_rep = lax.rem(device, n_rep) == my_rep
        same_column = lax.rem(lax.div(device, n_rep), PLANE) == lax.rem(my_row, PLANE)
        first = jnp.logical_and(jnp.logical_and(same_rep, same_column), device != me)
        second = jnp.logical_and(same_rep, jnp.logical_not(same_column))
        return first, second

    @pl.loop(0, reducers)
    def _(step):
        reducer = lax.rem(my_reducer + 1 + step, reducers)
        piece = gathered.at[reducer]

        @pl.when(mine(reducer)[0])
        def _():
            settle(piece, gather_sem.at[reducer])
            for hop in range(1, PLANE):
                row = lax.div(my_row, PLANE) * PLANE + lax.rem(my_row + hop, PLANE)
                remote(piece, piece, pass_sem.at[reducer, hop], gather_sem.at[reducer], row, my_rep).start()
            remote(piece, piece, pass_sem.at[reducer, 0], gather_sem.at[reducer], my_row, other_rep).start()

    settle(grad_in, receive_sem.at[4])
    all_rows = column(requests[...], 0).astype(jnp.int32)
    grads = unpack(grad_in[...]).astype(jnp.bfloat16)
    half = entity_ref.shape[0]

    @pl.loop(0, half // step_rows, unroll=2)
    def _(step):
        first = pl.multiple_of(step * step_rows, step_rows)
        lane = lax.broadcasted_iota(jnp.int32, (all_rows.shape[0], step_rows), 1) + first + my_rep * half
        place = (all_rows == lane).astype(jnp.float32).astype(jnp.bfloat16)
        entity_ref[pl.ds(first, step_rows), :] = dot(place, grads, 0, 0).astype(jnp.bfloat16)

    entity_copy = pltpu.make_async_copy(entity_ref, entity_hbm, local_sem.at[6])
    entity_copy.start()

    @pl.loop(0, reducers)
    def _(step):
        reducer = lax.rem(my_reducer + 1 + step, reducers)
        piece = gathered.at[reducer]

        @pl.when(mine(reducer)[1])
        def _():
            settle(piece, gather_sem.at[reducer])
            remote(piece, piece, pass_sem.at[reducer, 0], gather_sem.at[reducer], my_row, other_rep).start()

    @pl.loop(0, reducers // 2, unroll=4)
    def _(pair):
        halves = []
        for reducer in (2 * pair, 2 * pair + 1):

            @pl.when(lax.rem(reducer * stride, n_rep) != my_rep)
            def _():
                settle(gathered.at[reducer], gather_sem.at[reducer])

            rows = gathered[reducer].astype(jnp.float32)
            halves.append(jnp.concatenate([rows[:, :TILE, :], rows[:, TILE:, :]], axis=2))
        first = pl.multiple_of(pair * 2 * TILE, 2 * TILE)
        relation_out[:, pl.ds(first, 2 * TILE), :] = jnp.concatenate(halves, axis=1).astype(jnp.bfloat16)

    settle(head_ref.at[pl.ds(0, n_rows - 1)], send_sem.at[0])
    settle(head_ref, send_sem.at[1])
    settle(served.at[pl.ds(0, n_rows - 1)], send_sem.at[2])
    settle(op_out.at[pl.ds(0, reducers - 1)], send_sem.at[3])

    @pl.when(jnp.logical_not(reducing))
    def _():
        settle(op_out.at[0], send_sem.at[3])

    settle(grad_in.at[pl.ds(0, devices - 1)], send_sem.at[4])

    @pl.when(reducing)
    def _():
        for step in range(PLANE):
            settle(gathered.at[my_reducer], fan_sem.at[step])

        @pl.loop(1, n_rows // PLANE)
        def _(step):
            settle(gathered.at[my_reducer], fan_sem.at[PLANE + step])

    @pl.loop(0, reducers)
    def _(reducer):
        first, second = mine(reducer)

        @pl.when(jnp.logical_or(first, second))
        def _():
            settle(gathered.at[reducer], pass_sem.at[reducer, 0])

        @pl.when(first)
        def _():
            for hop in range(1, PLANE):
                settle(gathered.at[reducer], pass_sem.at[reducer, hop])

    entity_copy.wait()


def shards(
    entity_table, relation_ops, need_rows, send_offsets, source_ids, target_ids, negative_ids, relation_ids
):
    n_rows, n_rep = lax.axis_size("rows"), lax.axis_size("rep")
    devices = n_rows * n_rep
    need = need_rows[0, 0]
    capacity = need.shape[1]
    blocks, edges = source_ids.shape[2:]
    relations, width, _ = relation_ops.shape
    reducers = width // TILE
    scale = (relations / (edges * blocks * devices)) ** 0.5
    packed = (2 * TILE, LANES)
    slots = n_rows * capacity
    hbm = pl.BlockSpec(memory_space=pltpu.HBM)
    smem = pl.BlockSpec(memory_space=pltpu.SMEM)
    entity_shape = (entity_table.shape[0] // n_rep, width)
    entity_grad, relation_grad = pl.pallas_call(
        functools.partial(kernel, n_rows, n_rep, scale),
        out_shape=(
            jax.ShapeDtypeStruct(entity_shape, jnp.bfloat16),
            jax.ShapeDtypeStruct(relation_ops.shape, jnp.bfloat16),
        ),
        in_specs=[smem, smem] + [hbm] * 6,
        out_specs=(hbm, pl.BlockSpec(memory_space=pltpu.VMEM)),
        scratch_shapes=[
            pltpu.VMEM((capacity, n_rows), jnp.int32),
            pltpu.VMEM((blocks, edges), jnp.int32),
            pltpu.VMEM((blocks, edges), jnp.int32),
            pltpu.VMEM((blocks, negative_ids.shape[-1]), jnp.int32),
            pltpu.VMEM((n_rows, 1, LANES), jnp.int32),
            pltpu.VMEM((slots, LANES), jnp.int32),
            pltpu.VMEM(entity_shape, jnp.bfloat16),
            pltpu.VMEM(entity_table.shape, jnp.bfloat16),
            pltpu.VMEM(relation_ops.shape, jnp.bfloat16),
            pltpu.VMEM((devices, 1, LANES), jnp.int32),
            pltpu.VMEM((n_rows, *packed), jnp.bfloat16),
            pltpu.VMEM((n_rows, *packed), jnp.bfloat16),
            pltpu.VMEM((n_rows, *packed), jnp.bfloat16),
            pltpu.VMEM((devices, *packed), jnp.bfloat16),
            pltpu.VMEM((reducers, blocks, *packed), jnp.bfloat16),
            pltpu.VMEM((devices, blocks, *packed), jnp.bfloat16),
            pltpu.VMEM((blocks, devices, 1, LANES), jnp.float32),
            pltpu.VMEM((reducers, relations, *packed), jnp.bfloat16),
            pltpu.VMEM((blocks, slots, slots), jnp.float32),
            pltpu.VMEM((blocks, TILE, slots), jnp.float32),
            pltpu.VMEM((slots, width), jnp.float32),
            pltpu.SemaphoreType.DMA((7,)),
            pltpu.SemaphoreType.DMA((5,)),
            pltpu.SemaphoreType.DMA((5,)),
            pltpu.SemaphoreType.DMA((reducers,)),
            pltpu.SemaphoreType.DMA((PLANE + n_rows // PLANE,)),
            pltpu.SemaphoreType.DMA((reducers, PLANE)),
        ],
        compiler_params=pltpu.CompilerParams(
            collective_id=0, has_side_effects=True, vmem_limit_bytes=64 * 1024 * 1024 - 16384
        ),
    )(
        relation_ids[0, 0], send_offsets[0, 0], need.T, source_ids[0, 0], target_ids[0, 0], negative_ids[0, 0],
        entity_table, relation_ops,
    )
    return entity_grad, relation_grad.astype(jnp.float32)


def solution(mesh):
    return jax.shard_map(
        shards,
        mesh=mesh,
        in_specs=(
            P("rows", None),
            P(),
            P("rows", "rep", None, None),
            P("rows", "rep", None),
            P("rows", "rep", None, None),
            P("rows", "rep", None, None),
            P("rows", "rep", None, None),
            P("rows", "rep", None),
        ),
        out_specs=(P(("rows", "rep"), None), P()),
        check_vma=False,
    )
```
